128 devices in a mesh: row: 8 (over x, core), col: 16 (over y, z).
Axes of the slice: x: 4, y: 4, z: 4, core: 2. Of those that a mesh axis runs over, the one named last changes fastest.
Arguments:
- factor: bfloat16 [65536, 256], P(('row', 'col')), may hold values from -6 to 6
- relation_cores: float32 [2, 256, 256], replicated, may hold values from -6 to 6
- block_coords: int32 [2, 8, 16, 2, 96], P(None, 'row', 'col'), may hold values from 0 to 63, as said below
- block_values: int32 [2, 8, 16, 96, 128, 128], P(None, 'row', 'col'), may hold values from 0 to 3
- block_counts: int32 [2, 8, 16], P(None, 'row', 'col'), may hold values from 12 to 96, as said below
Outputs:
- factor_next: bfloat16 [65536, 256], P(('row', 'col'))
- cores_next: float32 [2, 256, 256], replicated
The draws below stay inside these ranges and needn't reach their ends.
Inputs may be any that keep to these rules, and one draw needn't show every extreme that they name: block_coords[k, r, c, 0, s] is a row block below 64 and block_coords[k, r, c, 1, s] a column block below 32; the 96 slots of one list name distinct blocks. Only the first block_counts[k, r, c] slots of a list are live; in every layer some grid cell has 96 live slots.
All inputs are finite; a program needn't handle non-finite values.
Results may differ from the reference program's by a relative error of at most 0.0054.
Values may be sent and summed in bfloat16 or wider, within the bound.
A program may use at most 192 MiB of HBM per device.

```python
import math
import jax
import jax.numpy as jnp
from jax import lax

RANK = 256
BLK = 128
LAYERS = 2
PIECE = 512
NBLK = 96
NODES = 65536
ROWB = 64
COLB = 32
N_ROW = 8
N_COL = 16


def draw_block_coords(key, part):
    key = jax.random.fold_in(key, 11)
    list_total = LAYERS * N_ROW * N_COL
    sub_keys = jax.random.split(key, list_total)
    col_total = N_ROW * PIECE // BLK
    cell_total = N_COL * PIECE // BLK * col_total

    def pick_slots(sub_key):
        return jax.random.permutation(sub_key, cell_total)[:NBLK]
    chosen = jax.vmap(pick_slots)(sub_keys).astype(jnp.int32)
    row_part = chosen // col_total
    col_part = chosen % col_total
    stacked = jnp.stack([row_part, col_part], axis=1)
    return stacked.reshape(LAYERS, N_ROW, N_COL, 2, NBLK).astype(jnp.int32)


def draw_block_counts(key, part):
    key = jax.random.fold_in(key, 23)
    base_key, busy_key = jax.random.split(key)
    counts = NBLK // 8 + jax.random.randint(base_key, (LAYERS, N_ROW * N_COL), 0, 3 * NBLK // 8 + 1)
    busiest = jax.random.randint(busy_key, (LAYERS, 1), 0, N_ROW * N_COL)
    device_ids = jnp.arange(N_ROW * N_COL)[None, :]
    counts = jnp.where(device_ids == busiest, NBLK, counts)
    return counts.reshape(LAYERS, N_ROW, N_COL).astype(jnp.int32)


def touch_ends(values, key, least, top_value):
    extent = values.shape
    spot = [jax.random.randint(jax.random.fold_in(key, axis), (), 0, extent[axis]) for axis in range(len(extent))]
    values = values.at[tuple(spot)].set(least)
    longest = extent.index(max(extent))
    spot[longest] = (spot[longest] + 1) % extent[longest]
    return values.at[tuple(spot)].set(top_value)


def shard_levels(rng, shape, shards, low, largest):
    level, own = 1.0, jax.random.fold_in(rng, 6)
    for dim, parts in shards:
        heights = jnp.exp(jax.random.uniform(jax.random.fold_in(own, dim), (parts,), jnp.float32, low / len(shards), largest / len(shards)))
        level = level * jnp.repeat(heights, shape[dim] // parts).reshape([-1 if axis == dim else 1 for axis in range(len(shape))])
    return level


def normal_values(own_key, dims, deviation, most, cuts=(), kind=jnp.bfloat16):
    drawn = jax.random.normal(own_key, dims, jnp.float32) * deviation
    if len(cuts) > 0:
        drawn = shard_levels(own_key, dims, cuts, -0.22, 0.18) * drawn
    return jnp.clip(drawn, min=-most, max=most).astype(kind)


def setup_inputs(seed: int = 0) -> dict:
    keys = jax.random.split(jax.random.key(seed), 6)
    factor = normal_values(keys[0], (NODES, RANK), 1.0, 6.0, ((0, 128),))
    relation_cores = normal_values(keys[1], (LAYERS, RANK, RANK), 1.0, 6.0, (), jnp.float32)
    block_coords = draw_block_coords(jax.random.fold_in(keys[5], 71), 0)
    block_values = touch_ends(jax.random.randint(keys[3], (LAYERS, N_ROW, N_COL, NBLK, BLK, BLK), 0, 4), jax.random.fold_in(keys[3], 1), 0, 3).astype(jnp.int32)
    block_counts = draw_block_counts(jax.random.fold_in(keys[5], 71), 0)
    return {"factor": factor, "relation_cores": relation_cores, "block_coords": block_coords, "block_values": block_values, "block_counts": block_counts}


step_factor = 0.25
step_core = 4.0

def group_terms(row_slabs, col_slabs, block_data, live_mask, layer_index):
    offset = (1 + layer_index) * RANK
    own_rows = row_slabs[:, :, :RANK].astype(jnp.float32)
    forward_rows = row_slabs[:, :, offset:offset + RANK].astype(jnp.float32)
    own_cols = col_slabs[:, :, :RANK].astype(jnp.float32)
    backward_cols = col_slabs[:, :, offset:offset + RANK].astype(jnp.float32)
    highest = lax.Precision.HIGHEST
    predicted = jnp.einsum('gar,gbr->gab', forward_rows, own_cols, precision=highest)
    residual = ((predicted - block_data) * live_mask[:, None, None]).astype(jnp.bfloat16).astype(jnp.float32)
    shared = jnp.einsum('gab,gbr->gar', residual, own_cols, precision=highest).astype(jnp.bfloat16).astype(jnp.float32)
    row_term = jnp.einsum('gab,gbr->gar', residual, backward_cols, precision=highest)
    col_term = jnp.einsum('gab,gar->gbr', residual, forward_rows, precision=highest)
    core_term = jnp.einsum('gar,gas->rs', own_rows, shared, precision=highest) * (1.0 / RANK)
    return (row_term, col_term, core_term)

def reference(factor, relation_cores, block_coords, block_values, block_counts):
    core_low = relation_cores.astype(jnp.bfloat16)
    inverse_rank = 1.0 / RANK
    forward = [(jnp.dot(factor, core_low[layer_index], preferred_element_type=jnp.float32) * inverse_rank).astype(jnp.bfloat16) for layer_index in range(LAYERS)]
    backward = [(jnp.dot(factor, core_low[layer_index].T, preferred_element_type=jnp.float32) * inverse_rank).astype(jnp.bfloat16) for layer_index in range(LAYERS)]
    width_all = (1 + LAYERS) * RANK
    row_grid = jnp.concatenate([factor] + forward, axis=1).reshape(N_ROW, ROWB, BLK, width_all)
    col_grid = jnp.concatenate([factor] + backward, axis=1).reshape(N_ROW, N_COL, PIECE, width_all)
    col_grid = col_grid.transpose(1, 0, 2, 3).reshape(N_COL, COLB, BLK, width_all)
    row_grad = jnp.zeros((N_ROW, ROWB, BLK, RANK), jnp.float32)
    col_grad = jnp.zeros((N_COL, COLB, BLK, RANK), jnp.float32)
    core_parts = []
    for layer_index in range(LAYERS):

        def cell_step(cell_index, totals_now, layer_index=layer_index):
            cell_index = jnp.asarray(cell_index).astype(jnp.int32)
            row_pos = cell_index // N_COL
            col_pos = cell_index % N_COL
            coords = block_coords[layer_index, row_pos, col_pos]
            layer_values = block_values[layer_index, row_pos, col_pos]
            live_count = block_counts[layer_index, row_pos, col_pos]

            def group_step(group_index, running):
                row_acc, col_acc, core_acc = running
                first_slot = jnp.asarray(group_index).astype(jnp.int32) * 8
                row_index = lax.dynamic_slice_in_dim(coords[0], first_slot, 8).astype(jnp.int32)
                col_index = lax.dynamic_slice_in_dim(coords[1], first_slot, 8).astype(jnp.int32)
                block_data = lax.dynamic_slice_in_dim(layer_values, first_slot, 8, 0).astype(jnp.float32)
                live_mask = (first_slot + jnp.arange(8, dtype=jnp.int32) < live_count).astype(jnp.float32)
                row_term, col_term, core_term = group_terms(row_grid[row_pos, row_index], col_grid[col_pos, col_index], block_data, live_mask, layer_index)
                return (row_acc.at[row_pos, row_index].add(row_term), col_acc.at[col_pos, col_index].add(col_term), core_acc + core_term)
            group_total = (live_count + 7) // 8
            return lax.fori_loop(0, group_total, group_step, totals_now)
        row_grad, col_grad, core_layer = lax.fori_loop(0, N_ROW * N_COL, cell_step, (row_grad, col_grad, jnp.zeros((RANK, RANK), jnp.float32)))
        core_parts.append(core_layer)
    col_nodes = col_grad.reshape(N_COL, N_ROW, PIECE, RANK).transpose(1, 0, 2, 3).reshape(NODES, RANK)
    factor_gradient = row_grad.reshape(NODES, RANK) + col_nodes
    factor_next = (factor.astype(jnp.float32) - step_factor * factor_gradient).astype(jnp.bfloat16)
    cores_next = relation_cores - step_core / math.sqrt(N_ROW * N_COL * NBLK) * jnp.stack(core_parts)
    return (factor_next, cores_next)
```

```python
import math

import jax
import jax.numpy as jnp
from jax import lax
from jax.experimental import pallas as pl
from jax.experimental.pallas import tpu as pltpu
from jax.sharding import PartitionSpec as P

step_factor = 0.25
step_core = 4.0

RING = 4
GROUP = 4
DEPTH = 4
MESH = pl.DeviceIdType.MESH


class Place:
    def __init__(self):
        row = lax.axis_index("row")
        col = lax.axis_index("col")
        self.x, self.core = lax.div(row, 2), lax.rem(row, 2)
        self.y, self.z = lax.div(col, RING), lax.rem(col, RING)

    def shifted(self, dx=0, dy=0, dz=0, dcore=0):
        x = lax.rem(self.x + dx + RING, RING)
        y = lax.rem(self.y + dy + RING, RING)
        z = lax.rem(self.z + dz + RING, RING)
        core = lax.rem(self.core + dcore, 2)
        return x, y, z, core

    def device(self, **shift):
        x, y, z, core = self.shifted(**shift)
        return (x * 2 + core, y * RING + z)

    def row_piece(self, **shift):
        _, y, z, _ = self.shifted(**shift)
        return y * RING + z

    def col_piece(self, **shift):
        x, _, _, core = self.shifted(**shift)
        return x * 2 + core


def axes_of(half, a, b):
    return {"dy": a, "dz": b} if half == 0 else {"dy": b, "dz": a}


class Copies:
    def __init__(self, send_sems, recv_sems, local_sems):
        self.send_sems, self.recv_sems, self.local_sems = send_sems, recv_sems, local_sems
        self.sent, self.kept = [], 0

    def send(self, src, dst, device):
        number = len(self.sent)
        copy = pltpu.make_async_remote_copy(
            src_ref=src,
            dst_ref=dst,
            send_sem=self.send_sems.at[number],
            recv_sem=self.recv_sems.at[number],
            device_id=device,
            device_id_type=MESH,
        )
        copy.start()
        self.sent.append(copy)
        return copy

    def local(self, src, dst):
        copy = pltpu.make_async_copy(src, dst, self.local_sems.at[self.kept])
        self.kept += 1
        copy.start()
        return copy

    def finish(self):
        for copy in self.sent:
            copy.wait_send()


def greet(devices):
    barrier = pltpu.get_barrier_semaphore()
    for device in devices:
        pl.semaphore_signal(barrier, inc=1, device_id=device, device_id_type=MESH)
    pl.semaphore_wait(barrier, len(devices))


def rows(start, size):
    return pl.ds(pl.multiple_of(start, 16), size)


GATHER_SENDS = 40 + 8


def gather_kernel(factor_ref, row_ref, col_ref, send_sems, recv_sems, local_sems):
    here = Place()
    piece = factor_ref.shape[0]
    half_rows, part_rows = piece // 2, piece // 4
    links = Copies(send_sems, recv_sems, local_sems)
    greet(
        [here.device(dx=d) for d in (1, -1)]
        + [here.device(dy=d) for d in (1, -1)]
        + [here.device(dz=d) for d in (1, -1)]
        + [here.device(dcore=1)]
    )

    def region(half, a, b, part=None):
        start = here.row_piece(**axes_of(half, a, b)) * piece + half * half_rows
        if part is None:
            return row_ref.at[rows(start, half_rows)]
        return row_ref.at[rows(start + part * part_rows, part_rows)]

    def own(half):
        return factor_ref.at[pl.ds(half * half_rows, half_rows)]

    def col_region(dx, dcore, half=None):
        start = here.col_piece(dx=dx, dcore=dcore) * piece
        if half is None:
            return col_ref.at[rows(start, piece)]
        return col_ref.at[rows(start + half * half_rows, half_rows)]

    def first(half, sign):
        return here.device(**axes_of(half, sign, 0))

    def second(half, sign):
        return here.device(**axes_of(half, 0, sign))

    halves = (0, 1)
    along, ahead, back = {}, {}, {}
    for half in halves:
        for sign in (1, -1):
            along[half, sign] = links.send(own(half), region(half, 0, 0), first(half, sign))
        for sign in (1, -1):
            ahead[half, 0, sign] = links.send(own(half), region(half, 0, 0), second(half, sign))
    col_along = {
        sign: links.send(factor_ref, col_region(0, 0), here.device(dx=sign)) for sign in (1, -1)
    }
    sibling = here.device(dcore=1)
    across = [links.send(factor_ref, col_region(0, 0), sibling)]
    kept = [links.local(factor_ref, row_ref.at[rows(here.row_piece() * piece, piece)])]
    kept.append(links.local(factor_ref, col_region(0, 0)))

    def spread(half, a):
        for sign in (1, -1):
            ahead[half, a, sign] = links.send(region(half, a, 0), region(half, a, 0), second(half, sign))

    def pass_on(half, a):
        for sign in (1, -1):
            ahead[half, a, sign].wait_recv()
            part = 0 if sign == 1 else 1
            spot = region(half, a, -sign, part)
            back[half, a, sign] = links.send(spot, spot, second(half, sign))

    far = {}
    for sign in (1, -1):
        for half in halves:
            along[half, sign].wait_recv()
            part = 0 if sign == 1 else 1
            spot = region(half, -sign, 0, part)
            far[half, sign] = links.send(spot, spot, first(half, sign))
            spread(half, -sign)
    col_far = {}
    for sign in (1, -1):
        col_along[sign].wait_recv()
        spot = col_region(-sign, 0, 0 if sign == 1 else 1)
        col_far[sign] = links.send(spot, spot, here.device(dx=sign))
        across.append(links.send(col_region(-sign, 0), col_region(-sign, 0), sibling))
    for half in halves:
        pass_on(half, 0)
    for half in halves:
        for sign in (1, -1):
            far[half, sign].wait_recv()
        spread(half, 2)
    for sign in (1, -1):
        col_far[sign].wait_recv()
    across.append(links.send(col_region(2, 0), col_region(2, 0), sibling))
    for a in (-1, 1, 2):
        for half in halves:
            pass_on(half, a)
    for copy in back.values():
        copy.wait_recv()
    for copy in across:
        copy.wait_recv()
    for copy in kept:
        copy.wait()
    links.finish()


def gather(factor):
    piece, width = factor.shape
    return pl.pallas_call(
        gather_kernel,
        out_shape=(
            jax.ShapeDtypeStruct((RING * RING * piece, width), factor.dtype),
            jax.ShapeDtypeStruct((RING * 2 * piece, width), factor.dtype),
        ),
        in_specs=[pl.BlockSpec(memory_space=pl.ANY)],
        out_specs=(pl.BlockSpec(memory_space=pl.ANY), pl.BlockSpec(memory_space=pl.ANY)),
        scratch_shapes=[
            pltpu.SemaphoreType.DMA((GATHER_SENDS,)),
            pltpu.SemaphoreType.DMA((GATHER_SENDS,)),
            pltpu.SemaphoreType.DMA((2,)),
        ],
        compiler_params=pltpu.CompilerParams(collective_id=0, has_side_effects=True),
        name="gather_factor",
    )(factor)


def dot_nn(left, right):
    return jnp.dot(left, right, preferred_element_type=jnp.float32)


def dot_nt(left, right):
    return lax.dot_general(left, right, (((1,), (1,)), ((), ())), preferred_element_type=jnp.float32)


def dot_tn(left, right):
    return lax.dot_general(left, right, (((0,), (0,)), ((), ())), preferred_element_type=jnp.float32)


def block_kernel(
    coords_ref,
    counts_ref,
    cores_ref,
    row_hbm,
    col_hbm,
    values_hbm,
    row_out,
    col_out,
    core_out,
    row_all,
    col_all,
    forward,
    shared,
    col_acc,
    values,
    row_stage,
    col_stage,
    row_sems,
    col_sem,
    value_sems,
    out_sems,
):
    layers, rank, _ = cores_ref.shape
    block = values.shape[-1]
    total_rows, total_cols = row_all.shape[0], col_all.shape[0]
    inverse_rank = 1.0 / rank
    load_rows = total_rows // row_sems.shape[0]

    def row_load(index):
        spot = pl.ds(pl.multiple_of(index * load_rows, load_rows), load_rows)
        return pltpu.make_async_copy(row_hbm.at[spot], row_all.at[spot], row_sems.at[index])

    col_load = pltpu.make_async_copy(col_hbm, col_all, col_sem)
    for index in range(row_sems.shape[0]):
        row_load(index).start()
    col_load.start()

    groups = [(counts_ref[layer] + GROUP - 1) // GROUP for layer in range(layers)]
    total = groups[0] + groups[1]

    def slot_of(step):
        layer = (step >= groups[0]).astype(jnp.int32)
        return layer, (step - layer * groups[0]) * GROUP

    def value_load(step):
        layer, first_slot = slot_of(step)
        place = lax.rem(step, DEPTH)
        return pltpu.make_async_copy(
            values_hbm.at[layer, 0, 0, pl.ds(first_slot, GROUP)], values.at[place], value_sems.at[place]
        )

    for step in range(DEPTH - 1):
        value_load(jnp.int32(step)).start()

    low = [cores_ref[layer].astype(jnp.bfloat16) for layer in range(layers)]
    low_wide = jnp.concatenate(low, axis=1)

    @pl.loop(0, row_sems.shape[0])
    def _(index):
        row_load(index).wait()
        start = pl.multiple_of(index * load_rows, load_rows)
        product = dot_nn(row_all[pl.ds(start, load_rows)], low_wide) * inverse_rank
        for layer in range(layers):
            forward[pl.ds(layer * total_rows + start, load_rows)] = product[
                :, layer * rank : (layer + 1) * rank
            ].astype(jnp.bfloat16)
            shared[pl.ds(layer * total_rows + start, load_rows)] = jnp.zeros((load_rows, rank), jnp.float32)
        part = total_cols // row_sems.shape[0]
        col_acc[pl.ds(pl.multiple_of(index * part, part), part)] = jnp.zeros((part, rank), jnp.float32)

    col_load.wait()

    @pl.loop(0, total)
    def _(step):
        value_load(step).wait()

        @pl.when(step + DEPTH - 1 < total)
        def _():
            value_load(step + DEPTH - 1).start()

        layer, first_slot = slot_of(step)
        place = lax.rem(step, DEPTH)
        spots = []
        for slot in range(GROUP):
            row_block = coords_ref[layer * 2, first_slot + slot]
            col_block = coords_ref[layer * 2 + 1, first_slot + slot]
            row_start = pl.multiple_of(layer * total_rows + row_block * block, block)
            col_start = pl.multiple_of(col_block * block, block)
            spots.append((pl.ds(row_start, block), pl.ds(col_start, block)))
        residuals = []
        for slot in range(GROUP):
            row_spot, col_spot = spots[slot]
            predicted = dot_nt(forward[row_spot], col_all[col_spot])
            live = first_slot + slot < counts_ref[layer]
            residual = jnp.where(live, predicted - values[place, slot].astype(jnp.float32), 0.0)
            residuals.append(residual.astype(jnp.bfloat16))
        for slot in range(GROUP):
            row_spot, col_spot = spots[slot]
            shared[row_spot] += dot_nn(residuals[slot], col_all[col_spot])
            col_acc[col_spot] += dot_tn(residuals[slot], forward[row_spot])

    stage_rows = row_stage.shape[1]
    steps = total_rows // stage_rows
    core_out[...] = jnp.zeros_like(core_out)
    col_rows = total_cols // steps

    def row_store(index):
        place = lax.rem(index, 2)
        return pltpu.make_async_copy(
            row_stage.at[place],
            row_out.at[pl.ds(pl.multiple_of(index * stage_rows, stage_rows), stage_rows)],
            out_sems.at[place],
        )

    def col_store(index):
        place = lax.rem(index, 2)
        return pltpu.make_async_copy(
            col_stage.at[place],
            col_out.at[pl.ds(pl.multiple_of(index * col_rows, col_rows), col_rows)],
            out_sems.at[2 + place],
        )

    @pl.loop(0, steps)
    def _(index):
        place = lax.rem(index, 2)

        @pl.when(index >= 2)
        def _():
            row_store(index - 2).wait()
            col_store(index - 2).wait()

        start = pl.multiple_of(index * stage_rows, stage_rows)
        sums = [
            shared[pl.ds(layer * total_rows + start, stage_rows)].astype(jnp.bfloat16)
            for layer in range(layers)
        ]
        row_term = dot_nt(sums[0], low[0])
        for layer in range(1, layers):
            row_term += dot_nt(sums[layer], low[layer])
        row_stage[place] = (row_term * inverse_rank).astype(jnp.bfloat16)
        row_store(index).start()
        col_stage[place] = col_acc[pl.ds(pl.multiple_of(index * col_rows, col_rows), col_rows)].astype(
            jnp.bfloat16
        )
        col_store(index).start()
        own = row_all[pl.ds(start, stage_rows)]
        for layer in range(layers):
            core_out[pl.ds(layer * rank, rank)] += dot_tn(own, sums[layer])

    for index in (steps - 2, steps - 1):
        row_store(jnp.int32(index)).wait()
        col_store(jnp.int32(index)).wait()


def local_terms(coords, counts, cores, row_all, col_all, block_values):
    layers, rank, _ = cores.shape
    total_rows, total_cols = row_all.shape[0], col_all.shape[0]
    block = block_values.shape[-1]
    stage_rows = 1024
    steps = total_rows // stage_rows
    anywhere = pl.BlockSpec(memory_space=pl.ANY)
    return pl.pallas_call(
        block_kernel,
        out_shape=(
            jax.ShapeDtypeStruct((total_rows, rank), jnp.bfloat16),
            jax.ShapeDtypeStruct((total_cols, rank), jnp.bfloat16),
            jax.ShapeDtypeStruct((layers * rank, rank), jnp.float32),
        ),
        in_specs=[
            pl.BlockSpec(memory_space=pltpu.SMEM),
            pl.BlockSpec(memory_space=pltpu.SMEM),
            pl.BlockSpec(memory_space=pltpu.VMEM),
            anywhere,
            anywhere,
            anywhere,
        ],
        out_specs=(anywhere, anywhere, pl.BlockSpec(memory_space=pltpu.VMEM)),
        scratch_shapes=[
            pltpu.VMEM((total_rows, rank), jnp.bfloat16),
            pltpu.VMEM((total_cols, rank), jnp.bfloat16),
            pltpu.VMEM((layers * total_rows, rank), jnp.bfloat16),
            pltpu.VMEM((layers * total_rows, rank), jnp.float32),
            pltpu.VMEM((total_cols, rank), jnp.float32),
            pltpu.VMEM((DEPTH, GROUP, block, block), jnp.int32),
            pltpu.VMEM((2, stage_rows, rank), jnp.bfloat16),
            pltpu.VMEM((2, total_cols // steps, rank), jnp.bfloat16),
            pltpu.SemaphoreType.DMA((8,)),
            pltpu.SemaphoreType.DMA,
            pltpu.SemaphoreType.DMA((DEPTH,)),
            pltpu.SemaphoreType.DMA((4,)),
        ],
        compiler_params=pltpu.CompilerParams(vmem_limit_bytes=56 * 1024 * 1024),
        name="block_terms",
    )(coords, counts, cores, row_all, col_all, block_values)


REDUCE_SENDS = 60 + 10 + 20
REDUCE_LOCALS = 24 + 4 + 1
PASS, SIDE = {1: 0, -1: 1}, {1: 2, -1: 4}


def reduce_kernel(
    row_ref,
    col_ref,
    core_ref,
    grad_ref,
    core_total_ref,
    row_own,
    row_in,
    row_out,
    row_kept,
    col_own,
    col_pair,
    col_in,
    col_out,
    core_own,
    core_pair,
    core_x,
    core_y,
    core_z,
    core_mid,
    core_big,
    core_all,
    send_sems,
    recv_sems,
    local_sems,
):
    here = Place()
    piece, width = grad_ref.shape
    half_rows, part_rows = piece // 2, piece // 4
    links = Copies(send_sems, recv_sems, local_sems)
    others = [{"d" + axis: d} for axis in "xyz" for d in (1, 2, 3)]
    greet([here.device(**shift) for shift in others] + [here.device(dcore=1)])
    halves = (0, 1)

    def region(half, a, b, part=None):
        start = here.row_piece(**axes_of(half, a, b)) * piece + half * half_rows
        if part is None:
            return row_ref.at[rows(start, half_rows)]
        return row_ref.at[rows(start + part * part_rows, part_rows)]

    def first(half, sign):
        return here.device(**axes_of(half, sign, 0))

    def second(half, sign):
        return here.device(**axes_of(half, 0, sign))

    def wide(ref):
        return ref[...].astype(jnp.float32)

    def near(sign):
        return 0 if sign == 1 else 1

    sibling = here.device(dcore=1)
    rank = core_own.shape[0]

    other_layer = core_ref.at[rows((1 - here.core) * rank, rank)]
    core_swap = links.send(other_layer, core_pair, sibling)
    core_keep = links.local(core_ref.at[rows(here.core * rank, rank)], core_own)

    col_swap, col_keep = {}, {}
    for dx in (2, 1, -1, 0):
        slot = dx % RING
        spot = col_ref.at[rows(here.col_piece(dx=dx, dcore=1) * piece, piece)]
        col_swap[dx] = links.send(spot, col_pair.at[slot], sibling)
        spot = col_ref.at[rows(here.col_piece(dx=dx) * piece, piece)]
        col_keep[dx] = links.local(spot, col_own.at[slot])

    pass_in, side_in, kept = {}, {}, {}

    def send_far(a):
        for half in halves:
            for sign in (1, -1):
                pass_in[half, a, sign] = links.send(
                    region(half, a, 2, near(sign)), row_in.at[half, a % RING, PASS[sign]], second(half, sign)
                )

    def send_plain(a):
        for half in halves:
            for sign in (1, -1):
                part = 1 - near(sign)
                side_in[half, a, sign, part] = links.send(
                    region(half, a, sign, part), row_in.at[half, a % RING, SIDE[sign] + part], second(half, sign)
                )

    def load_own(a):
        for half in halves:
            for sign in (1, -1):
                part = near(sign)
                kept[half, a, sign] = links.local(
                    region(half, a, sign, part), row_own.at[half, a % RING, pl.ds(part * part_rows, part_rows)]
                )
            kept[half, a, 0] = links.local(
                region(half, a, 0), row_own.at[half, a % RING, pl.ds(half_rows, half_rows)]
            )

    def send_sum(a):
        for half in halves:
            for sign in (1, -1):
                part = near(sign)
                pass_in[half, a, sign].wait_recv()
                kept[half, a, sign].wait()
                arrived = wide(row_in.at[half, a % RING, PASS[sign]])
                mine = wide(row_own.at[half, a % RING, pl.ds(part * part_rows, part_rows)])
                out = row_out.at[half, a % RING, part]
                out[...] = (mine + arrived).astype(jnp.bfloat16)
                side_in[half, a, sign, part] = links.send(
                    out, row_in.at[half, a % RING, SIDE[sign] + part], second(half, sign)
                )

    def close(a):
        for half in halves:
            kept[half, a, 0].wait()
            for part in (0, 1):
                for sign in (1, -1):
                    side_in[half, a, sign, part].wait_recv()
                arrived = wide(row_in.at[half, a % RING, SIDE[1] + part]) + wide(
                    row_in.at[half, a % RING, SIDE[-1] + part]
                )
                mine = wide(row_own.at[half, a % RING, pl.ds(half_rows + part * part_rows, part_rows)])
                row_kept[half, a % RING, pl.ds(part * part_rows, part_rows)] = mine + arrived

    last_pass, last_in = {}, {}

    def last_out(half, slot, a, part):
        out = row_out.at[half, RING, slot]
        out[...] = row_kept[half, a % RING, pl.ds(part * part_rows, part_rows)].astype(jnp.bfloat16)
        return out

    def last_far():
        for half in halves:
            for sign in (1, -1):
                out = last_out(half, near(sign), 2, near(sign))
                last_pass[half, sign] = links.send(out, row_in.at[half, RING, PASS[sign]], first(half, sign))

    def last_plain(sign):
        for half in halves:
            part = 1 - near(sign)
            out = last_out(half, 2 + part, sign, part)
            last_in[half, sign, part] = links.send(
                out, row_in.at[half, RING, SIDE[sign] + part], first(half, sign)
            )

    def last_sum(sign):
        for half in halves:
            part = near(sign)
            last_pass[half, sign].wait_recv()
            total = row_kept[half, sign % RING, pl.ds(part * part_rows, part_rows)] + wide(
                row_in.at[half, RING, PASS[sign]]
            )
            out = row_out.at[half, RING, 4 + part]
            out[...] = total.astype(jnp.bfloat16)
            last_in[half, sign, part] = links.send(
                out, row_in.at[half, RING, SIDE[sign] + part], first(half, sign)
            )

    col_pass, col_side = {}, {}

    def col_sum(dx):
        col_swap[dx].wait_recv()
        col_keep[dx].wait()
        slot = dx % RING
        return wide(col_own.at[slot]) + wide(col_pair.at[slot])

    def half_of(part):
        return pl.ds(part * half_rows, half_rows)

    def col_far():
        col_out[0] = col_sum(2).astype(jnp.bfloat16)
        for sign in (1, -1):
            col_pass[sign] = links.send(
                col_out.at[0, half_of(near(sign))], col_in.at[PASS[sign]], here.device(dx=sign)
            )

    def col_plain(sign):
        total = col_sum(sign)
        slot = 1 if sign == 1 else 2
        col_own[sign % RING] = total.astype(jnp.bfloat16)
        part = 1 - near(sign)
        col_out[slot, half_of(part)] = total[part * half_rows : (part + 1) * half_rows].astype(jnp.bfloat16)
        col_side[sign, part] = links.send(
            col_out.at[slot, half_of(part)], col_in.at[SIDE[sign] + part], here.device(dx=sign)
        )

    def col_pass_on(sign):
        slot = 1 if sign == 1 else 2
        part = near(sign)
        col_pass[sign].wait_recv()
        pair = wide(col_own.at[sign % RING, half_of(part)])
        col_out[slot, half_of(part)] = (pair + wide(col_in.at[PASS[sign]])).astype(jnp.bfloat16)
        col_side[sign, part] = links.send(
            col_out.at[slot, half_of(part)], col_in.at[SIDE[sign] + part], here.device(dx=sign)
        )

    def col_close():
        total = col_sum(0)
        for part in (0, 1):
            for sign in (1, -1):
                col_side[sign, part].wait_recv()
            grad_ref[half_of(part)] = (
                total[part * half_rows : (part + 1) * half_rows]
                + wide(col_in.at[SIDE[1] + part])
                + wide(col_in.at[SIDE[-1] + part])
            )

    x_rows, y_rows = rank // RING, rank // RING // RING
    stage = {}

    def core_to_x():
        core_swap.wait_recv()
        core_keep.wait()
        core_own[...] += core_pair[...]
        for d in (2, 1, 3):
            chunk = lax.rem(here.x + d, RING)
            stage["x", d] = links.send(
                core_own.at[rows(chunk * x_rows, x_rows)], core_x.at[d], here.device(dx=d)
            )

    def core_to_y():
        for d in (1, 2, 3):
            stage["x", d].wait_recv()
        core_mid[...] = (
            core_own[rows(here.x * x_rows, x_rows)] + core_x[1] + core_x[2] + core_x[3]
        )
        for d in (2, 1, 3):
            chunk = lax.rem(here.y + d, RING)
            stage["y", d] = links.send(
                core_mid.at[rows(chunk * y_rows, y_rows)], core_y.at[d], here.device(dy=d)
            )

    def core_to_z():
        for d in (1, 2, 3):
            stage["y", d].wait_recv()
        core_z[here.z] = core_mid[rows(here.y * y_rows, y_rows)] + core_y[1] + core_y[2] + core_y[3]
        for d in (2, 1, 3):
            stage["z", d] = links.send(core_z.at[here.z], core_z.at[here.z], here.device(dz=d))

    def core_back_y():
        for d in (1, 2, 3):
            stage["z", d].wait_recv()
        spot = core_big.at[rows(here.x * x_rows + here.y * y_rows, y_rows)]
        spot[...] = (core_z[0] + core_z[1]) + (core_z[2] + core_z[3])
        for d in (2, 1, 3):
            stage["by", d] = links.send(spot, spot, here.device(dy=d))

    def core_back_x():
        for d in (1, 2, 3):
            stage["by", d].wait_recv()
        spot = core_big.at[rows(here.x * x_rows, x_rows)]
        for d in (2, 1, 3):
            stage["bx", d] = links.send(spot, spot, here.device(dx=d))

    def core_back_chip():
        for d in (1, 2, 3):
            stage["bx", d].wait_recv()
        stage["chip"] = links.send(core_big, core_all, sibling)

    def core_close():
        stage["chip"].wait_recv()
        core_total_ref[rows(here.core * rank, rank)] = core_big[...]
        core_total_ref[rows((1 - here.core) * rank, rank)] = core_all[...]

    send_far(2)
    send_far(1)
    send_plain(2)
    for a in (2, 1, -1, 0):
        load_own(a)
    core_to_x()
    col_far()
    col_plain(1)
    col_plain(-1)
    send_sum(2)
    send_far(-1)
    send_plain(1)
    core_to_y()
    send_sum(1)
    send_far(0)
    send_plain(-1)
    col_pass_on(1)
    col_pass_on(-1)
    close(2)
    last_far()
    core_to_z()
    send_sum(-1)
    send_plain(0)
    close(1)
    last_plain(1)
    core_back_y()
    send_sum(0)
    close(-1)
    last_plain(-1)
    core_back_x()
    last_sum(1)
    last_sum(-1)
    col_close()
    core_back_chip()
    close(0)
    core_close()
    for half in halves:
        for part in (0, 1):
            for sign in (1, -1):
                last_in[half, sign, part].wait_recv()
            spot = pl.ds(half * half_rows + part * part_rows, part_rows)
            grad_ref[spot] += (
                row_kept[half, 0, pl.ds(part * part_rows, part_rows)]
                + wide(row_in.at[half, RING, SIDE[1] + part])
                + wide(row_in.at[half, RING, SIDE[-1] + part])
            )
    links.finish()


def reduce(row_grad, col_grad, core_grad, piece):
    width = row_grad.shape[1]
    half_rows, part_rows = piece // 2, piece // 4
    rank = width
    low, full = jnp.bfloat16, jnp.float32
    anywhere = pl.BlockSpec(memory_space=pl.ANY)
    inside = pl.BlockSpec(memory_space=pltpu.VMEM)
    return pl.pallas_call(
        reduce_kernel,
        out_shape=(
            jax.ShapeDtypeStruct((piece, width), full),
            jax.ShapeDtypeStruct(core_grad.shape, full),
        ),
        in_specs=[anywhere] * 3,
        out_specs=(inside, inside),
        scratch_shapes=[
            pltpu.VMEM((2, RING, piece, width), low),
            pltpu.VMEM((2, RING + 1, 6, part_rows, width), low),
            pltpu.VMEM((2, RING + 1, 6, part_rows, width), low),
            pltpu.VMEM((2, RING, half_rows, width), full),
            pltpu.VMEM((RING, piece, width), low),
            pltpu.VMEM((RING, piece, width), low),
            pltpu.VMEM((6, half_rows, width), low),
            pltpu.VMEM((3, piece, width), low),
            pltpu.VMEM((rank, width), full),
            pltpu.VMEM((rank, width), full),
            pltpu.VMEM((RING, rank // 4, width), full),
            pltpu.VMEM((RING, rank // 16, width), full),
            pltpu.VMEM((RING, rank // 16, width), full),
            pltpu.VMEM((rank // 4, width), full),
            pltpu.VMEM((rank, width), full),
            pltpu.VMEM((rank, width), full),
            pltpu.SemaphoreType.DMA((REDUCE_SENDS,)),
            pltpu.SemaphoreType.DMA((REDUCE_SENDS,)),
            pltpu.SemaphoreType.DMA((REDUCE_LOCALS,)),
        ],
        compiler_params=pltpu.CompilerParams(
            collective_id=1, has_side_effects=True, vmem_limit_bytes=40 * 1024 * 1024
        ),
        name="reduce_terms",
    )(row_grad, col_grad, core_grad)


def on_device(factor, relation_cores, block_coords, block_values, block_counts):
    slot_count = block_values.shape[3]
    cells = lax.axis_size("row") * lax.axis_size("col")
    layers = relation_cores.shape[0]
    row_all, col_all = gather(factor)
    row_grad, col_grad, core_grad = local_terms(
        block_coords.reshape(layers * 2, slot_count),
        block_counts.reshape(layers),
        relation_cores,
        row_all,
        col_all,
        block_values,
    )
    gradient, core_total = reduce(row_grad, col_grad, core_grad, factor.shape[0])
    factor_next = (factor.astype(jnp.float32) - step_factor * gradient).astype(jnp.bfloat16)
    core_total = core_total.reshape(relation_cores.shape) * (1.0 / factor.shape[1])
    cores_next = relation_cores - step_core / math.sqrt(cells * slot_count) * core_total
    return (factor_next, cores_next)


def solution(mesh):
    placed = (
        P(("row", "col"), None),
        P(),
        P(None, "row", "col", None, None),
        P(None, "row", "col", None, None, None),
        P(None, "row", "col"),
    )
    return jax.shard_map(
        on_device,
        mesh=mesh,
        in_specs=placed,
        out_specs=(P(("row", "col"), None), P()),
        check_vma=False,
    )
```

```python
import math

import jax
import jax.numpy as jnp
from jax import lax
from jax.experimental import pallas as pl
from jax.experimental.pallas import tpu as pltpu
from jax.sharding import PartitionSpec as P

step_factor = 0.25
step_core = 4.0

RING = 4
GROUP = 16
DEPTH = 3
MESH = pl.DeviceIdType.MESH


class Place:
    def __init__(self):
        row = lax.axis_index("row")
        col = lax.axis_index("col")
        self.x, self.core = lax.div(row, 2), lax.rem(row, 2)
        self.y, self.z = lax.div(col, RING), lax.rem(col, RING)

    def shifted(self, dx=0, dy=0, dz=0, dcore=0):
        x = lax.rem(self.x + dx + RING, RING)
        y = lax.rem(self.y + dy + RING, RING)
        z = lax.rem(self.z + dz + RING, RING)
        core = lax.rem(self.core + dcore, 2)
        return x, y, z, core

    def device(self, **shift):
        x, y, z, core = self.shifted(**shift)
        return (x * 2 + core, y * RING + z)

    def row_piece(self, **shift):
        _, y, z, _ = self.shifted(**shift)
        return y * RING + z

    def col_piece(self, **shift):
        x, _, _, core = self.shifted(**shift)
        return x * 2 + core


def dot_nn(left, right):
    return jnp.dot(left, right, preferred_element_type=jnp.float32)


def dot_nt(left, right):
    return lax.dot_general(left, right, (((1,), (1,)), ((), ())), preferred_element_type=jnp.float32)


def dot_tn(left, right):
    return lax.dot_general(left, right, (((0,), (0,)), ((), ())), preferred_element_type=jnp.float32)


def axes_of(half, a, b):
    return {"dy": a, "dz": b} if half == 0 else {"dy": b, "dz": a}


class Copies:
    def __init__(self, send_sems, recv_sems, local_sems):
        self.send_sems, self.recv_sems, self.local_sems = send_sems, recv_sems, local_sems
        self.sent, self.kept = [], 0

    def send(self, src, dst, device):
        number = len(self.sent)
        copy = pltpu.make_async_remote_copy(
            src_ref=src,
            dst_ref=dst,
            send_sem=self.send_sems.at[number],
            recv_sem=self.recv_sems.at[number],
            device_id=device,
            device_id_type=MESH,
        )
        copy.start()
        self.sent.append(copy)
        return copy

    def local(self, src, dst):
        copy = pltpu.make_async_copy(src, dst, self.local_sems.at[self.kept])
        self.kept += 1
        copy.start()
        return copy

    def finish(self):
        for copy in self.sent:
            copy.wait_send()


def greet(devices):
    barrier = pltpu.get_barrier_semaphore()
    for device in devices:
        pl.semaphore_signal(barrier, inc=1, device_id=device, device_id_type=MESH)
    pl.semaphore_wait(barrier, len(devices))


def pinned(x):
    return pltpu.with_memory_space_constraint(x, pltpu.VMEM)


def rows(start, size):
    return pl.ds(pl.multiple_of(start, 16), size)


GATHER_SENDS = 40 + 8


def gather_kernel(
    factor_ref,
    cores_ref,
    row_ref,
    col_ref,
    forward_ref,
    shared_ref,
    acc_ref,
    cores,
    low,
    send_sems,
    recv_sems,
    local_sems,
):
    here = Place()
    piece = factor_ref.shape[0]
    half_rows, part_rows = piece // 2, piece // 4
    total_rows = row_ref.shape[0]
    layers, rank, _ = cores_ref.shape
    links = Copies(send_sems, recv_sems, local_sems)
    cores_in = links.local(cores_ref, cores)
    greet(
        [here.device(dx=d) for d in (1, -1)]
        + [here.device(dy=d) for d in (1, -1)]
        + [here.device(dz=d) for d in (1, -1)]
        + [here.device(dcore=1)]
    )

    def region(half, a, b, part=None):
        start = here.row_piece(**axes_of(half, a, b)) * piece + half * half_rows
        if part is None:
            return row_ref.at[rows(start, half_rows)]
        return row_ref.at[rows(start + part * part_rows, part_rows)]

    def own(half):
        return factor_ref.at[pl.ds(half * half_rows, half_rows)]

    def col_region(dx, dcore, half=None):
        start = here.col_piece(dx=dx, dcore=dcore) * piece
        if half is None:
            return col_ref.at[rows(start, piece)]
        return col_ref.at[rows(start + half * half_rows, half_rows)]

    def first(half, sign):
        return here.device(**axes_of(half, sign, 0))

    def second(half, sign):
        return here.device(**axes_of(half, 0, sign))

    halves = (0, 1)
    along, ahead, back = {}, {}, {}
    for half in halves:
        for sign in (1, -1):
            along[half, sign] = links.send(own(half), region(half, 0, 0), first(half, sign))
        for sign in (1, -1):
            ahead[half, 0, sign] = links.send(own(half), region(half, 0, 0), second(half, sign))
    col_along = {
        sign: links.send(factor_ref, col_region(0, 0), here.device(dx=sign)) for sign in (1, -1)
    }
    sibling = here.device(dcore=1)
    across = [links.send(factor_ref, col_region(0, 0), sibling)]
    kept = [links.local(factor_ref, row_ref.at[rows(here.row_piece() * piece, piece)])]
    kept.append(links.local(factor_ref, col_region(0, 0)))

    zero_rows = 512

    @pl.loop(0, shared_ref.shape[0] // zero_rows)
    def _(index):
        shared_ref[rows(index * zero_rows, zero_rows)] = jnp.zeros((zero_rows, rank), jnp.float32)

    @pl.loop(0, acc_ref.shape[0] // zero_rows)
    def _(index):
        acc_ref[rows(index * zero_rows, zero_rows)] = jnp.zeros((zero_rows, rank), jnp.float32)

    cores_in.wait()
    for layer in range(layers):
        low[:, layer * rank : (layer + 1) * rank] = cores[layer].astype(jnp.bfloat16)

    def widen(half, a, b):
        start = here.row_piece(**axes_of(half, a, b)) * piece + half * half_rows
        product = dot_nn(row_ref[rows(start, half_rows)], low[...]) * (1.0 / rank)
        for layer in range(layers):
            forward_ref[rows(layer * total_rows + start, half_rows)] = product[
                :, layer * rank : (layer + 1) * rank
            ].astype(jnp.bfloat16)

    def spread(half, a):
        for sign in (1, -1):
            ahead[half, a, sign] = links.send(region(half, a, 0), region(half, a, 0), second(half, sign))

    def pass_on(half, a):
        for sign in (1, -1):
            ahead[half, a, sign].wait_recv()
            part = 0 if sign == 1 else 1
            spot = region(half, a, -sign, part)
            back[half, a, sign] = links.send(spot, spot, second(half, sign))

    def pass_wide(half, a):
        for sign in (1, -1):
            widen(half, a, -sign)

    for copy in kept:
        copy.wait()
    for half in halves:
        widen(half, 0, 0)
    far = {}
    for sign in (1, -1):
        for half in halves:
            along[half, sign].wait_recv()
            part = 0 if sign == 1 else 1
            spot = region(half, -sign, 0, part)
            far[half, sign] = links.send(spot, spot, first(half, sign))
            spread(half, -sign)
    for sign in (1, -1):
        for half in halves:
            widen(half, -sign, 0)
    col_far = {}
    for sign in (1, -1):
        col_along[sign].wait_recv()
        spot = col_region(-sign, 0, 0 if sign == 1 else 1)
        col_far[sign] = links.send(spot, spot, here.device(dx=sign))
        across.append(links.send(col_region(-sign, 0), col_region(-sign, 0), sibling))
    for half in halves:
        pass_on(half, 0)
    for half in halves:
        pass_wide(half, 0)
    for half in halves:
        for sign in (1, -1):
            far[half, sign].wait_recv()
        spread(half, 2)
    for half in halves:
        widen(half, 2, 0)
    for sign in (1, -1):
        col_far[sign].wait_recv()
    across.append(links.send(col_region(2, 0), col_region(2, 0), sibling))
    for a in (-1, 1, 2):
        for half in halves:
            pass_on(half, a)
        for half in halves:
            pass_wide(half, a)
    for a in (0, -1, 1, 2):
        for half in halves:
            for sign in (1, -1):
                back[half, a, sign].wait_recv()
            widen(half, a, 2)
    for copy in across:
        copy.wait_recv()
    links.finish()


def gather(factor, cores):
    piece, width = factor.shape
    layers = cores.shape[0]
    row_shape, col_shape = (RING * RING * piece, width), (RING * 2 * piece, width)
    wide_shape = (layers * row_shape[0], width)
    anywhere, inside = pl.BlockSpec(memory_space=pl.ANY), pl.BlockSpec(memory_space=pltpu.VMEM)
    return pl.pallas_call(
        gather_kernel,
        out_shape=(
            pltpu.VMEM(row_shape, factor.dtype),
            pltpu.VMEM(col_shape, factor.dtype),
            pltpu.VMEM(wide_shape, jnp.bfloat16),
            pltpu.VMEM(wide_shape, jnp.float32),
            pltpu.VMEM(col_shape, jnp.float32),
        ),
        in_specs=[anywhere, anywhere],
        out_specs=(inside,) * 5,
        scratch_shapes=[
            pltpu.VMEM(cores.shape, jnp.float32),
            pltpu.VMEM((width, layers * width), jnp.bfloat16),
            pltpu.SemaphoreType.DMA((GATHER_SENDS,)),
            pltpu.SemaphoreType.DMA((GATHER_SENDS,)),
            pltpu.SemaphoreType.DMA((3,)),
        ],
        compiler_params=pltpu.CompilerParams(
            collective_id=0, has_side_effects=True, vmem_limit_bytes=8 * 1024 * 1024
        ),
        name="gather_factor",
    )(factor, cores)


def block_kernel(
    coords_ref,
    counts_ref,
    forward,
    col_all,
    values_hbm,
    shared_in,
    acc_in,
    shared,
    col_acc,
    values,
    value_sems,
):
    layers, block = 2, values.shape[-1]
    total_rows = forward.shape[0] // layers
    groups = [(counts_ref[layer] + GROUP - 1) // GROUP for layer in range(layers)]
    total = groups[0] + groups[1]

    def slot_of(step):
        layer = (step >= groups[0]).astype(jnp.int32)
        return layer, (step - layer * groups[0]) * GROUP

    def value_load(step):
        layer, first_slot = slot_of(step)
        place = lax.rem(step, DEPTH)
        return pltpu.make_async_copy(
            values_hbm.at[layer, 0, 0, pl.ds(first_slot, GROUP)], values.at[place], value_sems.at[place]
        )

    for step in range(DEPTH - 1):
        value_load(jnp.int32(step)).start()

    @pl.loop(0, total)
    def _(step):
        value_load(step).wait()

        @pl.when(step + DEPTH - 1 < total)
        def _():
            value_load(step + DEPTH - 1).start()

        layer, first_slot = slot_of(step)
        place = lax.rem(step, DEPTH)
        spots = []
        for slot in range(GROUP):
            row_block = coords_ref[layer * 2, first_slot + slot]
            col_block = coords_ref[layer * 2 + 1, first_slot + slot]
            row_start = pl.multiple_of(layer * total_rows + row_block * block, block)
            col_start = pl.multiple_of(col_block * block, block)
            spots.append((pl.ds(row_start, block), pl.ds(col_start, block)))
        residuals = []
        for slot in range(GROUP):
            row_spot, col_spot = spots[slot]
            predicted = dot_nt(forward[row_spot], col_all[col_spot])
            live = first_slot + slot < counts_ref[layer]
            residual = jnp.where(live, predicted - values[place, slot].astype(jnp.float32), 0.0)
            residuals.append(residual.astype(jnp.bfloat16))
        for slot in range(GROUP):
            row_spot, col_spot = spots[slot]
            shared[row_spot] += dot_nn(residuals[slot], col_all[col_spot])
            col_acc[col_spot] += dot_tn(residuals[slot], forward[row_spot])


def local_terms(coords, counts, forward, col_all, block_values, shared, col_acc):
    block = block_values.shape[-1]
    scalars, inside = pl.BlockSpec(memory_space=pltpu.SMEM), pl.BlockSpec(memory_space=pltpu.VMEM)
    return pl.pallas_call(
        block_kernel,
        out_shape=(pltpu.VMEM(shared.shape, jnp.float32), pltpu.VMEM(col_acc.shape, jnp.float32)),
        in_specs=[scalars, scalars, inside, inside, pl.BlockSpec(memory_space=pl.ANY), inside, inside],
        out_specs=(inside, inside),
        input_output_aliases={5: 0, 6: 1},
        scratch_shapes=[
            pltpu.VMEM((DEPTH, GROUP, block, block), jnp.int32),
            pltpu.SemaphoreType.DMA((DEPTH,)),
        ],
        compiler_params=pltpu.CompilerParams(vmem_limit_bytes=12 * 1024 * 1024),
        name="block_terms",
    )(coords, counts, forward, col_all, block_values, shared, col_acc)


REDUCE_SENDS = 60 + 10 + 20
PASS, SIDE = {1: 0, -1: 1}, {1: 2, -1: 4}


def reduce_kernel(
    shared_ref,
    acc_ref,
    row_ref,
    cores_ref,
    grad_ref,
    core_total_ref,
    cores,
    low,
    core_terms,
    row_in,
    row_out,
    row_kept,
    col_swap_out,
    col_own,
    col_pair,
    col_in,
    col_out,
    core_own,
    core_pair,
    core_x,
    core_y,
    core_z,
    core_mid,
    core_big,
    core_all,
    send_sems,
    recv_sems,
    local_sems,
):
    here = Place()
    piece, width = grad_ref.shape
    half_rows, part_rows = piece // 2, piece // 4
    total_rows = row_ref.shape[0]
    layers, rank, _ = cores_ref.shape
    links = Copies(send_sems, recv_sems, local_sems)
    cores_in = links.local(cores_ref, cores)
    others = [{"d" + axis: d} for axis in "xyz" for d in (1, 2, 3)]
    greet([here.device(**shift) for shift in others] + [here.device(dcore=1)])
    halves = (0, 1)

    cores_in.wait()
    for layer in range(layers):
        low[layer] = cores[layer].astype(jnp.bfloat16)

    def term(half, a, b, part=None):
        start = here.row_piece(**axes_of(half, a, b)) * piece + half * half_rows
        size = half_rows
        if part is not None:
            start, size = start + part * part_rows, part_rows
        total = None
        for layer in range(layers):
            sums = shared_ref[rows(layer * total_rows + start, size)].astype(jnp.bfloat16)
            product = dot_nt(sums, low[layer])
            total = product if total is None else total + product
        return total * (1.0 / rank)

    def first(half, sign):
        return here.device(**axes_of(half, sign, 0))

    def second(half, sign):
        return here.device(**axes_of(half, 0, sign))

    def wide(ref):
        return ref[...].astype(jnp.float32)

    def near(sign):
        return 0 if sign == 1 else 1

    sibling = here.device(dcore=1)
    pass_in, side_in, col_swap, stage = {}, {}, {}, {}

    def send_far(a):
        for half in halves:
            both = term(half, a, 2).astype(jnp.bfloat16)
            for sign in (1, -1):
                part = near(sign)
                out = row_out.at[half, a % RING, PASS[sign]]
                out[...] = both[part * part_rows : (part + 1) * part_rows]
                pass_in[half, a, sign] = links.send(
                    out, row_in.at[half, a % RING, PASS[sign]], second(half, sign)
                )

    def send_plain(a):
        for half in halves:
            for sign in (1, -1):
                part = 1 - near(sign)
                out = row_out.at[half, a % RING, SIDE[sign] + part]
                out[...] = term(half, a, sign, part).astype(jnp.bfloat16)
                side_in[half, a, sign, part] = links.send(
                    out, row_in.at[half, a % RING, SIDE[sign] + part], second(half, sign)
                )

    def send_sum(a):
        for half in halves:
            for sign in (1, -1):
                part = near(sign)
                mine = term(half, a, sign, part)
                pass_in[half, a, sign].wait_recv()
                arrived = wide(row_in.at[half, a % RING, PASS[sign]])
                out = row_out.at[half, a % RING, SIDE[sign] + part]
                out[...] = (mine + arrived).astype(jnp.bfloat16)
                side_in[half, a, sign, part] = links.send(
                    out, row_in.at[half, a % RING, SIDE[sign] + part], second(half, sign)
                )

    def close(a):
        for half in halves:
            mine = term(half, a, 0)
            for part in (0, 1):
                for sign in (1, -1):
                    side_in[half, a, sign, part].wait_recv()
                arrived = wide(row_in.at[half, a % RING, SIDE[1] + part]) + wide(
                    row_in.at[half, a % RING, SIDE[-1] + part]
                )
                row_kept[half, a % RING, pl.ds(part * part_rows, part_rows)] = (
                    mine[part * part_rows : (part + 1) * part_rows] + arrived
                )

    def send_swap(dx):
        slot = dx % RING
        out = col_swap_out.at[slot]
        out[...] = acc_ref[rows(here.col_piece(dx=dx, dcore=1) * piece, piece)].astype(jnp.bfloat16)
        col_swap[dx] = links.send(out, col_pair.at[slot], sibling)

    def core_start():
        core_terms[...] = jnp.zeros_like(core_terms)
        step_rows = 1024

        @pl.loop(0, total_rows // step_rows)
        def _(index):
            start = index * step_rows
            own = row_ref[rows(start, step_rows)]
            for layer in range(layers):
                sums = shared_ref[rows(layer * total_rows + start, step_rows)].astype(jnp.bfloat16)
                core_terms[pl.ds(layer * rank, rank)] += dot_tn(own, sums)

        stage["swap"] = links.send(core_terms.at[rows((1 - here.core) * rank, rank)], core_pair, sibling)

    last_pass, last_in = {}, {}

    def last_out(half, slot, a, part):
        out = row_out.at[half, RING, slot]
        out[...] = row_kept[half, a % RING, pl.ds(part * part_rows, part_rows)].astype(jnp.bfloat16)
        return out

    def last_far():
        for half in halves:
            for sign in (1, -1):
                out = last_out(half, near(sign), 2, near(sign))
                last_pass[half, sign] = links.send(out, row_in.at[half, RING, PASS[sign]], first(half, sign))

    def last_plain(sign):
        for half in halves:
            part = 1 - near(sign)
            out = last_out(half, 2 + part, sign, part)
            last_in[half, sign, part] = links.send(
                out, row_in.at[half, RING, SIDE[sign] + part], first(half, sign)
            )

    def last_sum(sign):
        for half in halves:
            part = near(sign)
            last_pass[half, sign].wait_recv()
            total = row_kept[half, sign % RING, pl.ds(part * part_rows, part_rows)] + wide(
                row_in.at[half, RING, PASS[sign]]
            )
            out = row_out.at[half, RING, 4 + part]
            out[...] = total.astype(jnp.bfloat16)
            last_in[half, sign, part] = links.send(
                out, row_in.at[half, RING, SIDE[sign] + part], first(half, sign)
            )

    col_pass, col_side = {}, {}

    def col_sum(dx):
        mine = acc_ref[rows(here.col_piece(dx=dx) * piece, piece)]
        col_swap[dx].wait_recv()
        return mine + wide(col_pair.at[dx % RING])

    def half_of(part):
        return pl.ds(part * half_rows, half_rows)

    def col_far():
        col_out[0] = col_sum(2).astype(jnp.bfloat16)
        for sign in (1, -1):
            col_pass[sign] = links.send(
                col_out.at[0, half_of(near(sign))], col_in.at[PASS[sign]], here.device(dx=sign)
            )

    def col_plain(sign):
        total = col_sum(sign)
        slot = 1 if sign == 1 else 2
        part = near(sign)
        col_own[slot - 1] = total[part * half_rows : (part + 1) * half_rows]
        part = 1 - near(sign)
        col_out[slot, half_of(part)] = total[part * half_rows : (part + 1) * half_rows].astype(jnp.bfloat16)
        col_side[sign, part] = links.send(
            col_out.at[slot, half_of(part)], col_in.at[SIDE[sign] + part], here.device(dx=sign)
        )

    def col_pass_on(sign):
        slot = 1 if sign == 1 else 2
        part = near(sign)
        col_pass[sign].wait_recv()
        col_out[slot, half_of(part)] = (col_own[slot - 1] + wide(col_in.at[PASS[sign]])).astype(jnp.bfloat16)
        col_side[sign, part] = links.send(
            col_out.at[slot, half_of(part)], col_in.at[SIDE[sign] + part], here.device(dx=sign)
        )

    def col_close():
        total = col_sum(0)
        for part in (0, 1):
            for sign in (1, -1):
                col_side[sign, part].wait_recv()
            grad_ref[half_of(part)] = (
                total[part * half_rows : (part + 1) * half_rows]
                + wide(col_in.at[SIDE[1] + part])
                + wide(col_in.at[SIDE[-1] + part])
            )

    x_rows, y_rows = rank // RING, rank // RING // RING

    def core_to_x():
        stage["swap"].wait_recv()
        core_own[...] = core_terms[rows(here.core * rank, rank)] + core_pair[...]
        for d in (2, 1, 3):
            chunk = lax.rem(here.x + d, RING)
            stage["x", d] = links.send(
                core_own.at[rows(chunk * x_rows, x_rows)], core_x.at[d], here.device(dx=d)
            )

    def core_to_y():
        for d in (1, 2, 3):
            stage["x", d].wait_recv()
        core_mid[...] = (
            core_own[rows(here.x * x_rows, x_rows)] + core_x[1] + core_x[2] + core_x[3]
        )
        for d in (2, 1, 3):
            chunk = lax.rem(here.y + d, RING)
            stage["y", d] = links.send(
                core_mid.at[rows(chunk * y_rows, y_rows)], core_y.at[d], here.device(dy=d)
            )

    def core_to_z():
        for d in (1, 2, 3):
            stage["y", d].wait_recv()
        core_z[here.z] = core_mid[rows(here.y * y_rows, y_rows)] + core_y[1] + core_y[2] + core_y[3]
        for d in (2, 1, 3):
            stage["z", d] = links.send(core_z.at[here.z], core_z.at[here.z], here.device(dz=d))

    def core_back_y():
        for d in (1, 2, 3):
            stage["z", d].wait_recv()
        spot = core_big.at[rows(here.x * x_rows + here.y * y_rows, y_rows)]
        spot[...] = (core_z[0] + core_z[1]) + (core_z[2] + core_z[3])
        for d in (2, 1, 3):
            stage["by", d] = links.send(spot, spot, here.device(dy=d))

    def core_back_x():
        for d in (1, 2, 3):
            stage["by", d].wait_recv()
        spot = core_big.at[rows(here.x * x_rows, x_rows)]
        for d in (2, 1, 3):
            stage["bx", d] = links.send(spot, spot, here.device(dx=d))

    def core_back_chip():
        for d in (1, 2, 3):
            stage["bx", d].wait_recv()
        stage["chip"] = links.send(core_big, core_all, sibling)

    def core_close():
        stage["chip"].wait_recv()
        core_total_ref[rows(here.core * rank, rank)] = core_big[...]
        core_total_ref[rows((1 - here.core) * rank, rank)] = core_all[...]

    send_far(2)
    send_swap(2)
    send_far(1)
    send_plain(2)
    for dx in (1, -1, 0):
        send_swap(dx)
    core_start()
    col_far()
    col_plain(1)
    col_plain(-1)
    send_sum(2)
    core_to_x()
    send_far(-1)
    send_plain(1)
    send_sum(1)
    core_to_y()
    send_far(0)
    send_plain(-1)
    col_pass_on(1)
    col_pass_on(-1)
    close(2)
    last_far()
    core_to_z()
    send_sum(-1)
    send_plain(0)
    close(1)
    last_plain(1)
    core_back_y()
    send_sum(0)
    close(-1)
    last_plain(-1)
    core_back_x()
    last_sum(1)
    last_sum(-1)
    col_close()
    core_back_chip()
    close(0)
    core_close()
    for half in halves:
        for part in (0, 1):
            for sign in (1, -1):
                last_in[half, sign, part].wait_recv()
            spot = pl.ds(half * half_rows + part * part_rows, part_rows)
            grad_ref[spot] += (
                row_kept[half, 0, pl.ds(part * part_rows, part_rows)]
                + wide(row_in.at[half, RING, SIDE[1] + part])
                + wide(row_in.at[half, RING, SIDE[-1] + part])
            )
    links.finish()


def reduce(shared, col_acc, row_all, cores, piece):
    width = row_all.shape[1]
    layers = cores.shape[0]
    half_rows, part_rows = piece // 2, piece // 4
    rank = width
    low, full = jnp.bfloat16, jnp.float32
    anywhere = pl.BlockSpec(memory_space=pl.ANY)
    inside = pl.BlockSpec(memory_space=pltpu.VMEM)
    return pl.pallas_call(
        reduce_kernel,
        out_shape=(
            jax.ShapeDtypeStruct((piece, width), full),
            jax.ShapeDtypeStruct((layers * rank, width), full),
        ),
        in_specs=[inside, inside, inside, anywhere],
        out_specs=(inside, inside),
        scratch_shapes=[
            pltpu.VMEM(cores.shape, full),
            pltpu.VMEM(cores.shape, low),
            pltpu.VMEM((layers * rank, width), full),
            pltpu.VMEM((2, RING + 1, 6, part_rows, width), low),
            pltpu.VMEM((2, RING + 1, 6, part_rows, width), low),
            pltpu.VMEM((2, RING, half_rows, width), full),
            pltpu.VMEM((RING, piece, width), low),
            pltpu.VMEM((2, half_rows, width), full),
            pltpu.VMEM((RING, piece, width), low),
            pltpu.VMEM((6, half_rows, width), low),
            pltpu.VMEM((3, piece, width), low),
            pltpu.VMEM((rank, width), full),
            pltpu.VMEM((rank, width), full),
            pltpu.VMEM((RING, rank // 4, width), full),
            pltpu.VMEM((RING, rank // 16, width), full),
            pltpu.VMEM((RING, rank // 16, width), full),
            pltpu.VMEM((rank // 4, width), full),
            pltpu.VMEM((rank, width), full),
            pltpu.VMEM((rank, width), full),
            pltpu.SemaphoreType.DMA((REDUCE_SENDS,)),
            pltpu.SemaphoreType.DMA((REDUCE_SENDS,)),
            pltpu.SemaphoreType.DMA((1,)),
        ],
        compiler_params=pltpu.CompilerParams(
            collective_id=1, has_side_effects=True, vmem_limit_bytes=28 * 1024 * 1024
        ),
        name="reduce_terms",
    )(shared, col_acc, row_all, cores)


def on_device(factor, relation_cores, block_coords, block_values, block_counts):
    slot_count = block_values.shape[3]
    cells = lax.axis_size("row") * lax.axis_size("col")
    layers = relation_cores.shape[0]
    row_all, col_all, forward, shared, col_acc = map(pinned, gather(factor, relation_cores))
    shared, col_acc = map(
        pinned,
        local_terms(
            block_coords.reshape(layers * 2, slot_count),
            block_counts.reshape(layers),
            forward,
            col_all,
            block_values,
            shared,
            col_acc,
        ),
    )
    gradient, core_total = reduce(shared, col_acc, row_all, relation_cores, factor.shape[0])
    factor_next = (factor.astype(jnp.float32) - step_factor * gradient).astype(jnp.bfloat16)
    core_total = core_total.reshape(relation_cores.shape) * (1.0 / factor.shape[1])
    cores_next = relation_cores - step_core / math.sqrt(cells * slot_count) * core_total
    return (factor_next, cores_next)


def solution(mesh):
    placed = (
        P(("row", "col"), None),
        P(),
        P(None, "row", "col", None, None),
        P(None, "row", "col", None, None, None),
        P(None, "row", "col"),
    )
    return jax.shard_map(
        on_device,
        mesh=mesh,
        in_specs=placed,
        out_specs=(P(("row", "col"), None), P()),
        check_vma=False,
    )
```

```python
import math

import jax
import jax.numpy as jnp
from jax import lax
from jax.experimental import pallas as pl
from jax.experimental.pallas import tpu as pltpu
from jax.sharding import PartitionSpec as P

step_factor = 0.25
step_core = 4.0

RING = 4
GROUP = 16
DEPTH = 3
MESH = pl.DeviceIdType.MESH


class Place:
    def __init__(self):
        row = lax.axis_index("row")
        col = lax.axis_index("col")
        self.x, self.core = lax.div(row, 2), lax.rem(row, 2)
        self.y, self.z = lax.div(col, RING), lax.rem(col, RING)

    def shifted(self, dx=0, dy=0, dz=0, dcore=0):
        x = lax.rem(self.x + dx + RING, RING)
        y = lax.rem(self.y + dy + RING, RING)
        z = lax.rem(self.z + dz + RING, RING)
        core = lax.rem(self.core + dcore, 2)
        return x, y, z, core

    def device(self, **shift):
        x, y, z, core = self.shifted(**shift)
        return (x * 2 + core, y * RING + z)

    def row_piece(self, **shift):
        _, y, z, _ = self.shifted(**shift)
        return y * RING + z

    def col_piece(self, **shift):
        x, _, _, core = self.shifted(**shift)
        return x * 2 + core


def dot_nn(left, right):
    return jnp.dot(left, right, preferred_element_type=jnp.float32)


def dot_nt(left, right):
    return lax.dot_general(left, right, (((1,), (1,)), ((), ())), preferred_element_type=jnp.float32)


def dot_tn(left, right):
    return lax.dot_general(left, right, (((0,), (0,)), ((), ())), preferred_element_type=jnp.float32)


def axes_of(half, a, b):
    return {"dy": a, "dz": b} if half == 0 else {"dy": b, "dz": a}


class Copies:
    def __init__(self, send_sems, recv_sems, local_sems):
        self.send_sems, self.recv_sems, self.local_sems = send_sems, recv_sems, local_sems
        self.sent, self.kept = [], 0

    def send(self, src, dst, device):
        number = len(self.sent)
        copy = pltpu.make_async_remote_copy(
            src_ref=src,
            dst_ref=dst,
            send_sem=self.send_sems.at[number],
            recv_sem=self.recv_sems.at[number],
            device_id=device,
            device_id_type=MESH,
        )
        copy.start()
        self.sent.append(copy)
        return copy

    def local(self, src, dst):
        copy = pltpu.make_async_copy(src, dst, self.local_sems.at[self.kept])
        self.kept += 1
        copy.start()
        return copy

    def finish(self):
        for copy in self.sent:
            copy.wait_send()


def greet(devices, meanwhile=None):
    barrier = pltpu.get_barrier_semaphore()
    for device in devices:
        pl.semaphore_signal(barrier, inc=1, device_id=device, device_id_type=MESH)
    if meanwhile is not None:
        meanwhile()
    pl.semaphore_wait(barrier, len(devices))


def outside(x):
    return pltpu.with_memory_space_constraint(x, pltpu.HBM)


def pinned(x):
    return pltpu.with_memory_space_constraint(x, pltpu.VMEM)


def rows(start, size):
    return pl.ds(pl.multiple_of(start, 128 if size % 128 == 0 else 16), size)


GATHER_SENDS = 40 + 8


def gather_kernel(
    factor_ref,
    cores_ref,
    turned_ref,
    col_ref,
    forward_ref,
    shared_ref,
    acc_ref,
    row_ref,
    cores,
    low,
    send_sems,
    recv_sems,
    local_sems,
):
    here = Place()
    piece = factor_ref.shape[0]
    half_rows, part_rows = piece // 2, piece // 4
    total_rows = row_ref.shape[0]
    layers, rank, _ = cores_ref.shape
    links = Copies(send_sems, recv_sems, local_sems)
    cores_in = links.local(cores_ref, cores)
    greet(
        [here.device(dx=d) for d in (1, -1)]
        + [here.device(dy=d) for d in (1, -1)]
        + [here.device(dz=d) for d in (1, -1)]
        + [here.device(dcore=1)]
    )

    def region(half, a, b, part=None):
        start = here.row_piece(**axes_of(half, a, b)) * piece + half * half_rows
        if part is None:
            return row_ref.at[rows(start, half_rows)]
        return row_ref.at[rows(start + part * part_rows, part_rows)]

    def own(half):
        return factor_ref.at[pl.ds(half * half_rows, half_rows)]

    def col_region(dx, dcore, half=None):
        start = here.col_piece(dx=dx, dcore=dcore) * piece
        if half is None:
            return col_ref.at[rows(start, piece)]
        return col_ref.at[rows(start + half * half_rows, half_rows)]

    def first(half, sign):
        return here.device(**axes_of(half, sign, 0))

    def second(half, sign):
        return here.device(**axes_of(half, 0, sign))

    halves = (0, 1)
    along, ahead, back = {}, {}, {}
    for half in halves:
        for sign in (1, -1):
            along[half, sign] = links.send(own(half), region(half, 0, 0), first(half, sign))
        for sign in (1, -1):
            ahead[half, 0, sign] = links.send(own(half), region(half, 0, 0), second(half, sign))
    col_along = {
        sign: links.send(factor_ref, col_region(0, 0), here.device(dx=sign)) for sign in (1, -1)
    }
    sibling = here.device(dcore=1)
    across = [links.send(factor_ref, col_region(0, 0), sibling)]
    kept = [links.local(factor_ref, row_ref.at[rows(here.row_piece() * piece, piece)])]
    kept.append(links.local(factor_ref, col_region(0, 0)))

    zero_rows = 512

    @pl.loop(0, shared_ref.shape[0] // zero_rows)
    def _(index):
        shared_ref[rows(index * zero_rows, zero_rows)] = jnp.zeros((zero_rows, rank), jnp.float32)

    @pl.loop(0, acc_ref.shape[0] // zero_rows)
    def _(index):
        acc_ref[rows(index * zero_rows, zero_rows)] = jnp.zeros((zero_rows, rank), jnp.float32)

    cores_in.wait()
    for layer in range(layers):
        low[:, layer * rank : (layer + 1) * rank] = cores[layer].astype(jnp.bfloat16)

    def widen(half, a, b):
        start = here.row_piece(**axes_of(half, a, b)) * piece + half * half_rows
        arrived = row_ref[rows(start, half_rows)]
        turned_ref[:, rows(start, half_rows)] = arrived.T
        product = dot_nn(arrived, low[...]) * (1.0 / rank)
        for layer in range(layers):
            forward_ref[rows(layer * total_rows + start, half_rows)] = product[
                :, layer * rank : (layer + 1) * rank
            ].astype(jnp.bfloat16)

    def spread(half, a):
        for sign in (1, -1):
            ahead[half, a, sign] = links.send(region(half, a, 0), region(half, a, 0), second(half, sign))

    def pass_on(half, a):
        for sign in (1, -1):
            ahead[half, a, sign].wait_recv()
            part = 0 if sign == 1 else 1
            spot = region(half, a, -sign, part)
            back[half, a, sign] = links.send(spot, spot, second(half, sign))

    def pass_wide(half, a):
        for sign in (1, -1):
            widen(half, a, -sign)

    for copy in kept:
        copy.wait()
    for half in halves:
        widen(half, 0, 0)
    far = {}
    for sign in (1, -1):
        for half in halves:
            along[half, sign].wait_recv()
            part = 0 if sign == 1 else 1
            spot = region(half, -sign, 0, part)
            far[half, sign] = links.send(spot, spot, first(half, sign))
            spread(half, -sign)
    for sign in (1, -1):
        for half in halves:
            widen(half, -sign, 0)
    col_far = {}
    for sign in (1, -1):
        col_along[sign].wait_recv()
        spot = col_region(-sign, 0, 0 if sign == 1 else 1)
        col_far[sign] = links.send(spot, spot, here.device(dx=sign))
        across.append(links.send(col_region(-sign, 0), col_region(-sign, 0), sibling))
    for half in halves:
        pass_on(half, 0)
    for half in halves:
        pass_wide(half, 0)
    for half in halves:
        for sign in (1, -1):
            far[half, sign].wait_recv()
        spread(half, 2)
    for half in halves:
        widen(half, 2, 0)
    for sign in (1, -1):
        col_far[sign].wait_recv()
    across.append(links.send(col_region(2, 0), col_region(2, 0), sibling))
    for a in (-1, 1, 2):
        for half in halves:
            pass_on(half, a)
        for half in halves:
            pass_wide(half, a)
    for a in (0, -1, 1, 2):
        for half in halves:
            for sign in (1, -1):
                back[half, a, sign].wait_recv()
            widen(half, a, 2)
    for copy in across:
        copy.wait_recv()
    links.finish()


def gather(factor, cores):
    piece, width = factor.shape
    layers = cores.shape[0]
    row_shape, col_shape = (RING * RING * piece, width), (RING * 2 * piece, width)
    wide_shape = (layers * row_shape[0], width)
    anywhere, inside = pl.BlockSpec(memory_space=pl.ANY), pl.BlockSpec(memory_space=pltpu.VMEM)
    return pl.pallas_call(
        gather_kernel,
        out_shape=(
            pltpu.VMEM(row_shape[::-1], factor.dtype),
            pltpu.VMEM(col_shape, factor.dtype),
            pltpu.VMEM(wide_shape, jnp.bfloat16),
            pltpu.VMEM(wide_shape, jnp.float32),
            pltpu.VMEM(col_shape, jnp.float32),
        ),
        in_specs=[anywhere, anywhere],
        out_specs=(inside,) * 5,
        scratch_shapes=[
            pltpu.VMEM(row_shape, factor.dtype),
            pltpu.VMEM(cores.shape, jnp.float32),
            pltpu.VMEM((width, layers * width), jnp.bfloat16),
            pltpu.SemaphoreType.DMA((GATHER_SENDS,)),
            pltpu.SemaphoreType.DMA((GATHER_SENDS,)),
            pltpu.SemaphoreType.DMA((3,)),
        ],
        compiler_params=pltpu.CompilerParams(
            collective_id=0, has_side_effects=True, vmem_limit_bytes=8 * 1024 * 1024
        ),
        name="gather_factor",
    )(factor, cores)


def block_kernel(
    coords_hbm,
    counts_hbm,
    forward,
    col_all,
    values_hbm,
    shared_in,
    acc_in,
    shared,
    col_acc,
    values,
    coords_ref,
    counts_ref,
    value_sems,
    scalar_sems,
):
    layers, block = 2, values.shape[-1]
    total_rows = forward.shape[0] // layers
    coords_in = pltpu.make_async_copy(coords_hbm, coords_ref, scalar_sems.at[0])
    counts_in = pltpu.make_async_copy(counts_hbm, counts_ref, scalar_sems.at[1])
    counts_in.start()
    coords_in.start()
    counts_in.wait()
    groups = [(counts_ref[layer] + GROUP - 1) // GROUP for layer in range(layers)]
    total = groups[0] + groups[1]

    def slot_of(step):
        layer = (step >= groups[0]).astype(jnp.int32)
        return layer, (step - layer * groups[0]) * GROUP

    def value_load(step):
        layer, first_slot = slot_of(step)
        place = lax.rem(step, DEPTH)
        return pltpu.make_async_copy(
            values_hbm.at[layer, 0, 0, pl.ds(first_slot, GROUP)], values.at[place], value_sems.at[place]
        )

    for step in range(DEPTH - 1):

        @pl.when(step < total)
        def _():
            value_load(jnp.int32(step)).start()

    coords_in.wait()

    @pl.loop(0, total)
    def _(step):
        value_load(step).wait()

        @pl.when(step + DEPTH - 1 < total)
        def _():
            value_load(step + DEPTH - 1).start()

        layer, first_slot = slot_of(step)
        place = lax.rem(step, DEPTH)
        spots = []
        for slot in range(GROUP):
            row_block = coords_ref[layer * 2, first_slot + slot]
            col_block = coords_ref[layer * 2 + 1, first_slot + slot]
            row_start = pl.multiple_of(layer * total_rows + row_block * block, block)
            col_start = pl.multiple_of(col_block * block, block)
            spots.append((pl.ds(row_start, block), pl.ds(col_start, block)))
        residuals = []
        for slot in range(GROUP):
            row_spot, col_spot = spots[slot]
            predicted = dot_nt(forward[row_spot], col_all[col_spot])
            live = first_slot + slot < counts_ref[layer]
            residual = jnp.where(live, predicted - values[place, slot].astype(jnp.float32), 0.0)
            residuals.append(residual.astype(jnp.bfloat16))
        for slot in range(GROUP):
            row_spot, col_spot = spots[slot]
            shared[row_spot] += dot_nn(residuals[slot], col_all[col_spot])
            col_acc[col_spot] += dot_tn(residuals[slot], forward[row_spot])


def local_terms(coords, counts, forward, col_all, block_values, shared, col_acc):
    block = block_values.shape[-1]
    scalars, inside = pl.BlockSpec(memory_space=pl.ANY), pl.BlockSpec(memory_space=pltpu.VMEM)
    return pl.pallas_call(
        block_kernel,
        out_shape=(pltpu.VMEM(shared.shape, jnp.float32), pltpu.VMEM(col_acc.shape, jnp.float32)),
        in_specs=[scalars, scalars, inside, inside, pl.BlockSpec(memory_space=pl.ANY), inside, inside],
        out_specs=(inside, inside),
        input_output_aliases={5: 0, 6: 1},
        scratch_shapes=[
            pltpu.VMEM((DEPTH, GROUP, block, block), jnp.int32),
            pltpu.SMEM(coords.shape, jnp.int32),
            pltpu.SMEM(counts.shape, jnp.int32),
            pltpu.SemaphoreType.DMA((DEPTH,)),
            pltpu.SemaphoreType.DMA((2,)),
        ],
        compiler_params=pltpu.CompilerParams(vmem_limit_bytes=12 * 1024 * 1024),
        name="block_terms",
    )(coords, counts, forward, col_all, block_values, shared, col_acc)


REDUCE_SENDS = 60 + 10 + 20
ROW_ORDER = (4, 5, 3, 2, 6, 7, 1)
PASS, SIDE = {1: 0, -1: 1}, {1: 2, -1: 4}


def reduce_kernel(
    shared_ref,
    acc_ref,
    turned_ref,
    cores_ref,
    grad_ref,
    core_total_ref,
    cores,
    low,
    core_terms,
    row_in,
    row_out,
    row_kept,
    col_swap_out,
    col_own,
    col_pair,
    col_in,
    col_out,
    core_out,
    core_in,
    core_y,
    core_z,
    core_all,
    send_sems,
    recv_sems,
    local_sems,
):
    here = Place()
    piece, width = grad_ref.shape
    half_rows, part_rows = piece // 2, piece // 4
    total_rows = turned_ref.shape[1]
    layers, rank, _ = cores_ref.shape
    links = Copies(send_sems, recv_sems, local_sems)
    cores_in = links.local(cores_ref, cores)
    row_count = 2 * RING
    row, col = lax.axis_index("row"), lax.axis_index("col")

    def row_device(d):
        return (lax.rem(row + d, row_count), col)

    partners = [row_device(d) for d in range(1, row_count)]
    partners += [here.device(**{"d" + axis: d}) for axis in "yz" for d in (1, 2, 3)]
    row_part = layers * rank // row_count

    def core_terms_here():
        core_terms[...] = jnp.zeros_like(core_terms)
        step_rows = 1024

        @pl.loop(0, total_rows // step_rows)
        def _(index):
            start = index * step_rows
            own = turned_ref[:, rows(start, step_rows)]
            for layer in range(layers):
                sums = shared_ref[rows(layer * total_rows + start, step_rows)].astype(jnp.bfloat16)
                core_terms[pl.ds(layer * rank, rank)] += dot_nn(own, sums)

        core_out[...] = core_terms[...].astype(jnp.bfloat16)

    greet(partners, core_terms_here)
    halves = (0, 1)
    cores_in.wait()
    for layer in range(layers):
        low[layer] = cores[layer].astype(jnp.bfloat16)

    def term(half, a, b, part=None):
        start = here.row_piece(**axes_of(half, a, b)) * piece + half * half_rows
        size = half_rows
        if part is not None:
            start, size = start + part * part_rows, part_rows
        total = None
        for layer in range(layers):
            sums = shared_ref[rows(layer * total_rows + start, size)].astype(jnp.bfloat16)
            product = dot_nt(sums, low[layer])
            total = product if total is None else total + product
        return total * (1.0 / rank)

    def first(half, sign):
        return here.device(**axes_of(half, sign, 0))

    def second(half, sign):
        return here.device(**axes_of(half, 0, sign))

    def wide(ref):
        return ref[...].astype(jnp.float32)

    def near(sign):
        return 0 if sign == 1 else 1

    sibling = here.device(dcore=1)
    pass_in, side_in, col_swap, stage = {}, {}, {}, {}

    def send_far(a):
        for half in halves:
            both = term(half, a, 2).astype(jnp.bfloat16)
            for sign in (1, -1):
                part = near(sign)
                out = row_out.at[half, a % RING, PASS[sign]]
                out[...] = both[part * part_rows : (part + 1) * part_rows]
                pass_in[half, a, sign] = links.send(
                    out, row_in.at[half, a % RING, PASS[sign]], second(half, sign)
                )

    def send_plain(a):
        for half in halves:
            for sign in (1, -1):
                part = 1 - near(sign)
                out = row_out.at[half, a % RING, SIDE[sign] + part]
                out[...] = term(half, a, sign, part).astype(jnp.bfloat16)
                side_in[half, a, sign, part] = links.send(
                    out, row_in.at[half, a % RING, SIDE[sign] + part], second(half, sign)
                )

    def send_sum(a):
        for half in halves:
            for sign in (1, -1):
                part = near(sign)
                mine = term(half, a, sign, part)
                pass_in[half, a, sign].wait_recv()
                arrived = wide(row_in.at[half, a % RING, PASS[sign]])
                out = row_out.at[half, a % RING, SIDE[sign] + part]
                out[...] = (mine + arrived).astype(jnp.bfloat16)
                side_in[half, a, sign, part] = links.send(
                    out, row_in.at[half, a % RING, SIDE[sign] + part], second(half, sign)
                )

    def close(a):
        for half in halves:
            mine = term(half, a, 0)
            for part in (0, 1):
                for sign in (1, -1):
                    side_in[half, a, sign, part].wait_recv()
                arrived = wide(row_in.at[half, a % RING, SIDE[1] + part]) + wide(
                    row_in.at[half, a % RING, SIDE[-1] + part]
                )
                row_kept[half, a % RING, pl.ds(part * part_rows, part_rows)] = (
                    mine[part * part_rows : (part + 1) * part_rows] + arrived
                )

    def send_swap(dx):
        slot = dx % RING
        out = col_swap_out.at[slot]
        out[...] = acc_ref[rows(here.col_piece(dx=dx, dcore=1) * piece, piece)].astype(jnp.bfloat16)
        col_swap[dx] = links.send(out, col_pair.at[slot], sibling)

    def core_start():
        for d in ROW_ORDER:
            chunk = lax.rem(row + d, row_count)
            stage["row", d] = links.send(
                core_out.at[rows(chunk * row_part, row_part)], core_in.at[d], row_device(d)
            )

    last_pass, last_in = {}, {}

    def last_out(half, slot, a, part):
        out = row_out.at[half, RING, slot]
        out[...] = row_kept[half, a % RING, pl.ds(part * part_rows, part_rows)].astype(jnp.bfloat16)
        return out

    def last_far():
        for half in halves:
            for sign in (1, -1):
                out = last_out(half, near(sign), 2, near(sign))
                last_pass[half, sign] = links.send(out, row_in.at[half, RING, PASS[sign]], first(half, sign))

    def last_plain(sign):
        for half in halves:
            part = 1 - near(sign)
            out = last_out(half, 2 + part, sign, part)
            last_in[half, sign, part] = links.send(
                out, row_in.at[half, RING, SIDE[sign] + part], first(half, sign)
            )

    def last_sum(sign):
        for half in halves:
            part = near(sign)
            last_pass[half, sign].wait_recv()
            total = row_kept[half, sign % RING, pl.ds(part * part_rows, part_rows)] + wide(
                row_in.at[half, RING, PASS[sign]]
            )
            out = row_out.at[half, RING, 4 + part]
            out[...] = total.astype(jnp.bfloat16)
            last_in[half, sign, part] = links.send(
                out, row_in.at[half, RING, SIDE[sign] + part], first(half, sign)
            )

    col_pass, col_side = {}, {}

    def col_sum(dx):
        mine = acc_ref[rows(here.col_piece(dx=dx) * piece, piece)]
        col_swap[dx].wait_recv()
        return mine + wide(col_pair.at[dx % RING])

    def half_of(part):
        return pl.ds(part * half_rows, half_rows)

    def col_far():
        col_out[0] = col_sum(2).astype(jnp.bfloat16)
        for sign in (1, -1):
            col_pass[sign] = links.send(
                col_out.at[0, half_of(near(sign))], col_in.at[PASS[sign]], here.device(dx=sign)
            )

    def col_plain(sign):
        total = col_sum(sign)
        slot = 1 if sign == 1 else 2
        part = near(sign)
        col_own[slot - 1] = total[part * half_rows : (part + 1) * half_rows]
        part = 1 - near(sign)
        col_out[slot, half_of(part)] = total[part * half_rows : (part + 1) * half_rows].astype(jnp.bfloat16)
        col_side[sign, part] = links.send(
            col_out.at[slot, half_of(part)], col_in.at[SIDE[sign] + part], here.device(dx=sign)
        )

    def col_pass_on(sign):
        slot = 1 if sign == 1 else 2
        part = near(sign)
        col_pass[sign].wait_recv()
        col_out[slot, half_of(part)] = (col_own[slot - 1] + wide(col_in.at[PASS[sign]])).astype(jnp.bfloat16)
        col_side[sign, part] = links.send(
            col_out.at[slot, half_of(part)], col_in.at[SIDE[sign] + part], here.device(dx=sign)
        )

    def col_close():
        total = col_sum(0)
        for part in (0, 1):
            for sign in (1, -1):
                col_side[sign, part].wait_recv()
            grad_ref[half_of(part)] = (
                total[part * half_rows : (part + 1) * half_rows]
                + wide(col_in.at[SIDE[1] + part])
                + wide(col_in.at[SIDE[-1] + part])
            )

    def core_to_y():
        for d in range(1, row_count):
            stage["row", d].wait_recv()
        total = core_terms[rows(row * row_part, row_part)]
        for d in range(1, row_count):
            total += wide(core_in.at[d])
        core_y[here.y] = total.astype(jnp.bfloat16)
        for d in (2, 1, 3):
            stage["y", d] = links.send(core_y.at[here.y], core_y.at[here.y], here.device(dy=d))

    def core_to_z():
        for d in (1, 2, 3):
            stage["y", d].wait_recv()
        total = (wide(core_y.at[0]) + wide(core_y.at[1])) + (wide(core_y.at[2]) + wide(core_y.at[3]))
        core_z[here.z] = total.astype(jnp.bfloat16)
        for d in (2, 1, 3):
            stage["z", d] = links.send(core_z.at[here.z], core_z.at[here.z], here.device(dz=d))

    def core_back_row():
        for d in (1, 2, 3):
            stage["z", d].wait_recv()
        spot = core_all.at[rows(row * row_part, row_part)]
        spot[...] = (wide(core_z.at[0]) + wide(core_z.at[1])) + (wide(core_z.at[2]) + wide(core_z.at[3]))
        for d in (2, 1, 3):
            stage["bx", d] = links.send(spot, spot, row_device(2 * d))
        stage["chip", 0] = links.send(spot, spot, sibling)

    def core_back_chip():
        for d in (1, 3, 2):
            stage["bx", d].wait_recv()
            from_row = lax.rem(row + 2 * (RING - d), row_count)
            spot = core_all.at[rows(from_row * row_part, row_part)]
            stage["chip", d] = links.send(spot, spot, sibling)

    def core_close():
        for d in range(RING):
            stage["chip", d].wait_recv()
        core_total_ref[...] = core_all[...]

    core_start()
    send_far(2)
    send_far(1)
    send_far(-1)
    send_far(0)
    send_swap(2)
    send_swap(1)
    send_swap(-1)
    send_swap(0)
    send_plain(2)
    core_to_y()
    send_sum(2)
    send_plain(1)
    col_far()
    col_plain(1)
    col_plain(-1)
    send_sum(1)
    core_to_z()
    send_plain(-1)
    send_plain(0)
    close(2)
    last_far()
    core_back_row()
    send_sum(-1)
    send_sum(0)
    close(1)
    last_plain(1)
    core_back_chip()
    col_pass_on(1)
    col_pass_on(-1)
    close(-1)
    last_plain(-1)
    last_sum(1)
    last_sum(-1)
    col_close()
    close(0)
    core_close()
    for half in halves:
        for part in (0, 1):
            for sign in (1, -1):
                last_in[half, sign, part].wait_recv()
            spot = pl.ds(half * half_rows + part * part_rows, part_rows)
            grad_ref[spot] += (
                row_kept[half, 0, pl.ds(part * part_rows, part_rows)]
                + wide(row_in.at[half, RING, SIDE[1] + part])
                + wide(row_in.at[half, RING, SIDE[-1] + part])
            )
    links.finish()


def reduce(shared, col_acc, turned, cores, piece):
    width = turned.shape[0]
    layers = cores.shape[0]
    half_rows, part_rows = piece // 2, piece // 4
    rank = width
    low, full = jnp.bfloat16, jnp.float32
    anywhere = pl.BlockSpec(memory_space=pl.ANY)
    inside = pl.BlockSpec(memory_space=pltpu.VMEM)
    return pl.pallas_call(
        reduce_kernel,
        out_shape=(
            jax.ShapeDtypeStruct((piece, width), full),
            jax.ShapeDtypeStruct((layers * rank, width), full),
        ),
        in_specs=[inside, inside, inside, anywhere],
        out_specs=(inside, inside),
        scratch_shapes=[
            pltpu.VMEM(cores.shape, full),
            pltpu.VMEM(cores.shape, low),
            pltpu.VMEM((layers * rank, width), full),
            pltpu.VMEM((2, RING + 1, 6, part_rows, width), low),
            pltpu.VMEM((2, RING + 1, 6, part_rows, width), low),
            pltpu.VMEM((2, RING, half_rows, width), full),
            pltpu.VMEM((RING, piece, width), low),
            pltpu.VMEM((2, half_rows, width), full),
            pltpu.VMEM((RING, piece, width), low),
            pltpu.VMEM((6, half_rows, width), low),
            pltpu.VMEM((3, piece, width), low),
            pltpu.VMEM((layers * rank, width), low),
            pltpu.VMEM((2 * RING, layers * rank // (2 * RING), width), low),
            pltpu.VMEM((RING, layers * rank // (2 * RING), width), low),
            pltpu.VMEM((RING, layers * rank // (2 * RING), width), low),
            pltpu.VMEM((layers * rank, width), full),
            pltpu.SemaphoreType.DMA((REDUCE_SENDS,)),
            pltpu.SemaphoreType.DMA((REDUCE_SENDS,)),
            pltpu.SemaphoreType.DMA((1,)),
        ],
        compiler_params=pltpu.CompilerParams(
            collective_id=1, has_side_effects=True, vmem_limit_bytes=18 * 1024 * 1024
        ),
        name="reduce_terms",
    )(shared, col_acc, turned, cores)


def on_device(factor, relation_cores, block_coords, block_values, block_counts):
    slot_count = block_values.shape[3]
    cells = lax.axis_size("row") * lax.axis_size("col")
    layers = relation_cores.shape[0]
    factor_far, cores_far = outside(factor), outside(relation_cores)
    turned, col_all, forward, shared, col_acc = map(pinned, gather(factor_far, cores_far))
    shared, col_acc = map(
        pinned,
        local_terms(
            outside(block_coords.reshape(layers * 2, slot_count)),
            outside(block_counts.reshape(layers)),
            forward,
            col_all,
            block_values,
            shared,
            col_acc,
        ),
    )
    gradient, core_total = reduce(shared, col_acc, turned, cores_far, factor.shape[0])
    factor_next = (factor.astype(jnp.float32) - step_factor * gradient).astype(jnp.bfloat16)
    core_total = core_total.reshape(relation_cores.shape) * (1.0 / factor.shape[1])
    cores_next = relation_cores - step_core / math.sqrt(cells * slot_count) * core_total
    return (factor_next, cores_next)


def solution(mesh):
    placed = (
        P(("row", "col"), None),
        P(),
        P(None, "row", "col", None, None),
        P(None, "row", "col", None, None, None),
        P(None, "row", "col"),
    )
    return jax.shard_map(
        on_device,
        mesh=mesh,
        in_specs=placed,
        out_specs=(P(("row", "col"), None), P()),
        check_vma=False,
    )
```

```python
import math

import jax
import jax.numpy as jnp
from jax import lax
from jax.experimental import pallas as pl
from jax.experimental.pallas import tpu as pltpu
from jax.sharding import PartitionSpec as P

step_factor = 0.25
step_core = 4.0

RING = 4
GROUP = 16
DEPTH = 3
MESH = pl.DeviceIdType.MESH


class Place:
    def __init__(self):
        row = lax.axis_index("row")
        col = lax.axis_index("col")
        self.x, self.core = lax.div(row, 2), lax.rem(row, 2)
        self.y, self.z = lax.div(col, RING), lax.rem(col, RING)

    def shifted(self, dx=0, dy=0, dz=0, dcore=0):
        x = lax.rem(self.x + dx + RING, RING)
        y = lax.rem(self.y + dy + RING, RING)
        z = lax.rem(self.z + dz + RING, RING)
        core = lax.rem(self.core + dcore, 2)
        return x, y, z, core

    def device(self, **shift):
        x, y, z, core = self.shifted(**shift)
        return (x * 2 + core, y * RING + z)

    def row_piece(self, **shift):
        _, y, z, _ = self.shifted(**shift)
        return y * RING + z

    def col_piece(self, **shift):
        x, _, _, core = self.shifted(**shift)
        return x * 2 + core


def dot_nn(left, right):
    return jnp.dot(left, right, preferred_element_type=jnp.float32)


def dot_nt(left, right):
    return lax.dot_general(left, right, (((1,), (1,)), ((), ())), preferred_element_type=jnp.float32)


def dot_tn(left, right):
    return lax.dot_general(left, right, (((0,), (0,)), ((), ())), preferred_element_type=jnp.float32)


def axes_of(half, a, b):
    return {"dy": a, "dz": b} if half == 0 else {"dy": b, "dz": a}


class Copies:
    def __init__(self, send_sems, recv_sems, local_sems):
        self.send_sems, self.recv_sems, self.local_sems = send_sems, recv_sems, local_sems
        self.sent, self.kept, self.drained = [], 0, 0

    def send(self, src, dst, device):
        number = len(self.sent)
        copy = pltpu.make_async_remote_copy(
            src_ref=src,
            dst_ref=dst,
            send_sem=self.send_sems.at[number],
            recv_sem=self.recv_sems.at[number],
            device_id=device,
            device_id_type=MESH,
        )
        copy.start()
        self.sent.append(copy)
        return copy

    def local(self, src, dst):
        copy = pltpu.make_async_copy(src, dst, self.local_sems.at[self.kept])
        self.kept += 1
        copy.start()
        return copy

    def drain(self, keep=0):
        last = len(self.sent) - keep
        for copy in self.sent[self.drained : last]:
            copy.wait_send()
        self.drained = max(self.drained, last)


def greet(devices, meanwhile=None):
    barrier = pltpu.get_barrier_semaphore()
    for device in devices:
        pl.semaphore_signal(barrier, inc=1, device_id=device, device_id_type=MESH)
    if meanwhile is not None:
        meanwhile()
    pl.semaphore_wait(barrier, len(devices))


def outside(x):
    return pltpu.with_memory_space_constraint(x, pltpu.HBM)


def pinned(x):
    return pltpu.with_memory_space_constraint(x, pltpu.VMEM)


def rows(start, size):
    return pl.ds(pl.multiple_of(start, 128 if size % 128 == 0 else 16), size)


GATHER_SENDS = 60 + 8


def gather_kernel(
    factor_ref,
    cores_ref,
    turned_ref,
    col_ref,
    forward_ref,
    shared_ref,
    acc_ref,
    row_ref,
    cores,
    low,
    send_sems,
    recv_sems,
    local_sems,
):
    here = Place()
    piece = factor_ref.shape[0]
    half_rows, part_rows = piece // 2, piece // 4
    total_rows = row_ref.shape[0]
    layers, rank, _ = cores_ref.shape
    links = Copies(send_sems, recv_sems, local_sems)
    cores_in = links.local(cores_ref, cores)
    greet(
        [here.device(dx=d) for d in (1, -1)]
        + [here.device(dy=d) for d in (1, -1)]
        + [here.device(dz=d) for d in (1, -1)]
        + [here.device(dcore=1)]
    )

    def region(half, a, b, part=None):
        start = here.row_piece(**axes_of(half, a, b)) * piece + half * half_rows
        if part is None:
            return row_ref.at[rows(start, half_rows)]
        return row_ref.at[rows(start + part * part_rows, part_rows)]

    def col_region(dx, dcore, half=None):
        start = here.col_piece(dx=dx, dcore=dcore) * piece
        if half is None:
            return col_ref.at[rows(start, piece)]
        return col_ref.at[rows(start + half * half_rows, half_rows)]

    def first(half, sign):
        return here.device(**axes_of(half, sign, 0))

    def second(half, sign):
        return here.device(**axes_of(half, 0, sign))

    halves = (0, 1)
    along, ahead, far, back, col_along, col_far = {}, {}, {}, {}, {}, {}
    sibling = here.device(dcore=1)
    across = []

    def near(sign):
        return 0 if sign == 1 else 1

    def own(half, part):
        return factor_ref.at[pl.ds(half * half_rows + part * part_rows, part_rows)]

    def send_along(passed):
        for half in halves:
            for sign in (1, -1):
                part = near(sign) if passed else 1 - near(sign)
                along[half, sign, part] = links.send(
                    own(half, part), region(half, 0, 0, part), first(half, sign)
                )

    def send_own(passed):
        for half in halves:
            for sign in (1, -1):
                part = near(sign) if passed else 1 - near(sign)
                ahead[half, 0, sign, part] = links.send(
                    own(half, part), region(half, 0, 0, part), second(half, sign)
                )

    def spread(half, a, part):
        spot = region(half, a, 0, part)
        for sign in (1, -1) if part == 0 else (-1, 1):
            ahead[half, a, sign, part] = links.send(spot, spot, second(half, sign))

    def take_along(passed):
        for sign in (1, -1):
            part = near(sign) if passed else 1 - near(sign)
            for half in halves:
                along[half, sign, part].wait_recv()
                if passed:
                    spot = region(half, -sign, 0, part)
                    far[half, sign] = links.send(spot, spot, first(half, sign))
                spread(half, -sign, part)

    def take_far():
        for sign in (1, -1):
            for half in halves:
                far[half, sign].wait_recv()
                spread(half, 2, near(sign))

    def pass_on(a):
        for half in halves:
            for sign in (1, -1):
                part = near(sign)
                ahead[half, a, sign, part].wait_recv()
                spot = region(half, a, -sign, part)
                back[half, a, sign] = links.send(spot, spot, second(half, sign))

    def take_rest(a):
        for half in halves:
            for sign in (1, -1):
                ahead[half, a, sign, 1 - near(sign)].wait_recv()

    def take_back(a):
        for half in halves:
            for sign in (1, -1):
                back[half, a, sign].wait_recv()

    def widen(half, a, b):
        start = here.row_piece(**axes_of(half, a, b)) * piece + half * half_rows
        arrived = row_ref[rows(start, half_rows)]
        turned_ref[:, rows(start, half_rows)] = arrived.T
        product = dot_nn(arrived, low[...]) * (1.0 / rank)
        for layer in range(layers):
            forward_ref[rows(layer * total_rows + start, half_rows)] = product[
                :, layer * rank : (layer + 1) * rank
            ].astype(jnp.bfloat16)

    def widen_all(a, b):
        for half in halves:
            widen(half, a, b)

    def col_start():
        for sign in (1, -1):
            col_along[sign] = links.send(factor_ref, col_region(0, 0), here.device(dx=sign))
        across.append(links.send(factor_ref, col_region(0, 0), sibling))

    def col_pass():
        for sign in (1, -1):
            col_along[sign].wait_recv()
            spot = col_region(-sign, 0, near(sign))
            col_far[sign] = links.send(spot, spot, here.device(dx=sign))
            across.append(links.send(col_region(-sign, 0), col_region(-sign, 0), sibling))

    def col_end():
        for sign in (1, -1):
            col_far[sign].wait_recv()
        across.append(links.send(col_region(2, 0), col_region(2, 0), sibling))

    def prepare():
        zero_rows = 512

        @pl.loop(0, shared_ref.shape[0] // zero_rows)
        def _(index):
            shared_ref[rows(index * zero_rows, zero_rows)] = jnp.zeros((zero_rows, rank), jnp.float32)

        @pl.loop(0, acc_ref.shape[0] // zero_rows)
        def _(index):
            acc_ref[rows(index * zero_rows, zero_rows)] = jnp.zeros((zero_rows, rank), jnp.float32)

        cores_in.wait()
        for layer in range(layers):
            low[:, layer * rank : (layer + 1) * rank] = cores[layer].astype(jnp.bfloat16)
        for copy in kept:
            copy.wait()

    def drain():
        links.drain(4)

    def finish():
        for copy in across:
            copy.wait_recv()
        links.drain()

    kept = [
        links.local(factor_ref, row_ref.at[rows(here.row_piece() * piece, piece)]),
        links.local(factor_ref, col_region(0, 0)),
    ]
    send_along(True)
    send_along(False)
    send_own(True)
    send_own(False)
    col_start()
    prepare()
    widen_all(0,0)
    take_along(True)
    take_along(False)
    widen_all(-1,0)
    widen_all(1,0)
    col_pass()
    take_far()
    pass_on(0)
    widen_all(2,0)
    col_end()
    take_rest(0)
    widen_all(0,1)
    widen_all(0,-1)
    pass_on(-1)
    take_rest(-1)
    widen_all(-1,1)
    widen_all(-1,-1)
    pass_on(1)
    take_rest(1)
    widen_all(1,1)
    widen_all(1,-1)
    pass_on(2)
    take_rest(2)
    widen_all(2,1)
    widen_all(2,-1)
    take_back(0)
    widen_all(0,2)
    take_back(-1)
    widen_all(-1,2)
    take_back(1)
    widen_all(1,2)
    drain()
    take_back(2)
    widen_all(2,2)
    finish()

def gather(factor, cores):
    piece, width = factor.shape
    layers = cores.shape[0]
    row_shape, col_shape = (RING * RING * piece, width), (RING * 2 * piece, width)
    wide_shape = (layers * row_shape[0], width)
    anywhere, inside = pl.BlockSpec(memory_space=pl.ANY), pl.BlockSpec(memory_space=pltpu.VMEM)
    return pl.pallas_call(
        gather_kernel,
        out_shape=(
            pltpu.VMEM(row_shape[::-1], factor.dtype),
            pltpu.VMEM(col_shape, factor.dtype),
            pltpu.VMEM(wide_shape, jnp.bfloat16),
            pltpu.VMEM(wide_shape, jnp.float32),
            pltpu.VMEM(col_shape, jnp.float32),
        ),
        in_specs=[anywhere, anywhere],
        out_specs=(inside,) * 5,
        scratch_shapes=[
            pltpu.VMEM(row_shape, factor.dtype),
            pltpu.VMEM(cores.shape, jnp.float32),
            pltpu.VMEM((width, layers * width), jnp.bfloat16),
            pltpu.SemaphoreType.DMA((GATHER_SENDS,)),
            pltpu.SemaphoreType.DMA((GATHER_SENDS,)),
            pltpu.SemaphoreType.DMA((3,)),
        ],
        compiler_params=pltpu.CompilerParams(
            collective_id=0, has_side_effects=True, vmem_limit_bytes=8 * 1024 * 1024
        ),
        name="gather_factor",
    )(factor, cores)


def block_kernel(
    coords_hbm,
    counts_hbm,
    forward,
    col_all,
    values_hbm,
    shared_in,
    acc_in,
    shared,
    col_acc,
    values,
    coords_ref,
    counts_ref,
    value_sems,
    scalar_sems,
):
    layers, block = 2, values.shape[-1]
    total_rows = forward.shape[0] // layers
    coords_in = pltpu.make_async_copy(coords_hbm, coords_ref, scalar_sems.at[0])
    counts_in = pltpu.make_async_copy(counts_hbm, counts_ref, scalar_sems.at[1])
    counts_in.start()
    coords_in.start()
    counts_in.wait()
    groups = [(counts_ref[layer] + GROUP - 1) // GROUP for layer in range(layers)]
    total = groups[0] + groups[1]

    def slot_of(step):
        layer = (step >= groups[0]).astype(jnp.int32)
        return layer, (step - layer * groups[0]) * GROUP

    def value_load(step):
        layer, first_slot = slot_of(step)
        place = lax.rem(step, DEPTH)
        return pltpu.make_async_copy(
            values_hbm.at[layer, 0, 0, pl.ds(first_slot, GROUP)], values.at[place], value_sems.at[place]
        )

    for step in range(DEPTH - 1):

        @pl.when(step < total)
        def _():
            value_load(jnp.int32(step)).start()

    coords_in.wait()

    @pl.loop(0, total)
    def _(step):
        value_load(step).wait()

        @pl.when(step + DEPTH - 1 < total)
        def _():
            value_load(step + DEPTH - 1).start()

        layer, first_slot = slot_of(step)
        place = lax.rem(step, DEPTH)
        spots = []
        for slot in range(GROUP):
            row_block = coords_ref[layer * 2, first_slot + slot]
            col_block = coords_ref[layer * 2 + 1, first_slot + slot]
            row_start = pl.multiple_of(layer * total_rows + row_block * block, block)
            col_start = pl.multiple_of(col_block * block, block)
            spots.append((pl.ds(row_start, block), pl.ds(col_start, block)))
        residuals = []
        for slot in range(GROUP):
            row_spot, col_spot = spots[slot]
            predicted = dot_nt(forward[row_spot], col_all[col_spot])
            live = first_slot + slot < counts_ref[layer]
            residual = jnp.where(live, predicted - values[place, slot].astype(jnp.float32), 0.0)
            residuals.append(residual.astype(jnp.bfloat16))
        for slot in range(GROUP):
            row_spot, col_spot = spots[slot]
            shared[row_spot] += dot_nn(residuals[slot], col_all[col_spot])
            col_acc[col_spot] += dot_tn(residuals[slot], forward[row_spot])


def local_terms(coords, counts, forward, col_all, block_values, shared, col_acc):
    block = block_values.shape[-1]
    scalars, inside = pl.BlockSpec(memory_space=pl.ANY), pl.BlockSpec(memory_space=pltpu.VMEM)
    return pl.pallas_call(
        block_kernel,
        out_shape=(pltpu.VMEM(shared.shape, jnp.float32), pltpu.VMEM(col_acc.shape, jnp.float32)),
        in_specs=[scalars, scalars, inside, inside, pl.BlockSpec(memory_space=pl.ANY), inside, inside],
        out_specs=(inside, inside),
        input_output_aliases={5: 0, 6: 1},
        scratch_shapes=[
            pltpu.VMEM((DEPTH, GROUP, block, block), jnp.int32),
            pltpu.SMEM(coords.shape, jnp.int32),
            pltpu.SMEM(counts.shape, jnp.int32),
            pltpu.SemaphoreType.DMA((DEPTH,)),
            pltpu.SemaphoreType.DMA((2,)),
        ],
        compiler_params=pltpu.CompilerParams(vmem_limit_bytes=12 * 1024 * 1024),
        name="block_terms",
    )(coords, counts, forward, col_all, block_values, shared, col_acc)


REDUCE_SENDS = 60 + 10 + 20
ROW_ORDER = (4, 5, 3, 2, 6, 7, 1)
PASS, SIDE = {1: 0, -1: 1}, {1: 2, -1: 4}


def reduce_kernel(
    shared_ref,
    acc_ref,
    turned_ref,
    cores_ref,
    grad_ref,
    core_total_ref,
    cores,
    low,
    core_terms,
    row_in,
    row_out,
    row_kept,
    col_swap_out,
    col_own,
    col_pair,
    col_in,
    col_out,
    core_out,
    core_in,
    core_y,
    core_z,
    core_all,
    send_sems,
    recv_sems,
    local_sems,
):
    here = Place()
    piece, width = grad_ref.shape
    half_rows, part_rows = piece // 2, piece // 4
    total_rows = turned_ref.shape[1]
    layers, rank, _ = cores_ref.shape
    links = Copies(send_sems, recv_sems, local_sems)
    cores_in = links.local(cores_ref, cores)
    row_count = 2 * RING
    row, col = lax.axis_index("row"), lax.axis_index("col")

    def row_device(d):
        return (lax.rem(row + d, row_count), col)

    partners = [row_device(d) for d in range(1, row_count)]
    partners += [here.device(**{"d" + axis: d}) for axis in "yz" for d in (1, 2, 3)]
    row_part = layers * rank // row_count

    def core_terms_here():
        core_terms[...] = jnp.zeros_like(core_terms)
        step_rows = 8192

        @pl.loop(0, total_rows // step_rows)
        def _(index):
            start = index * step_rows
            own = turned_ref[:, rows(start, step_rows)]
            for layer in range(layers):
                sums = shared_ref[rows(layer * total_rows + start, step_rows)].astype(jnp.bfloat16)
                core_terms[pl.ds(layer * rank, rank)] += dot_nn(own, sums)

        core_out[...] = core_terms[...].astype(jnp.bfloat16)

    greet(partners, core_terms_here)
    halves = (0, 1)
    cores_in.wait()
    for layer in range(layers):
        low[layer] = cores[layer].astype(jnp.bfloat16)

    def term(half, a, b):
        start = here.row_piece(**axes_of(half, a, b)) * piece + half * half_rows
        total = None
        for layer in range(layers):
            sums = shared_ref[rows(layer * total_rows + start, half_rows)].astype(jnp.bfloat16)
            product = dot_nt(sums, low[layer])
            total = product if total is None else total + product
        return total * (1.0 / rank)

    def first(half, sign):
        return here.device(**axes_of(half, sign, 0))

    def second(half, sign):
        return here.device(**axes_of(half, 0, sign))

    def wide(ref):
        return ref[...].astype(jnp.float32)

    def quarter(part):
        return pl.ds(part * part_rows, part_rows)

    def near(sign):
        return 0 if sign == 1 else 1

    sibling = here.device(dcore=1)
    pass_in, side_in, col_swap, stage = {}, {}, {}, {}

    def send_far(a):
        for half in halves:
            both = term(half, a, 2).astype(jnp.bfloat16)
            for sign in (1, -1):
                part = near(sign)
                out = row_out.at[half, a % RING, PASS[sign]]
                out[...] = both[part * part_rows : (part + 1) * part_rows]
                pass_in[half, a, sign] = links.send(
                    out, row_in.at[half, a % RING, PASS[sign]], second(half, sign)
                )

    def send_plain(a):
        for half in halves:
            for sign in (1, -1):
                part = 1 - near(sign)
                both = term(half, a, sign)
                out = row_out.at[half, a % RING, SIDE[sign] + part]
                out[...] = both[part * part_rows : (part + 1) * part_rows].astype(jnp.bfloat16)
                row_kept[half, a % RING, quarter(1 - part)] = both[
                    (1 - part) * part_rows : (2 - part) * part_rows
                ]
                side_in[half, a, sign, part] = links.send(
                    out, row_in.at[half, a % RING, SIDE[sign] + part], second(half, sign)
                )

    def send_sum(a):
        for half in halves:
            for sign in (1, -1):
                part = near(sign)
                mine = row_kept[half, a % RING, quarter(part)]
                pass_in[half, a, sign].wait_recv()
                arrived = wide(row_in.at[half, a % RING, PASS[sign]])
                out = row_out.at[half, a % RING, SIDE[sign] + part]
                out[...] = (mine + arrived).astype(jnp.bfloat16)
                side_in[half, a, sign, part] = links.send(
                    out, row_in.at[half, a % RING, SIDE[sign] + part], second(half, sign)
                )

    def close(a):
        for half in halves:
            mine = term(half, a, 0)
            for part in (0, 1):
                for sign in (1, -1):
                    side_in[half, a, sign, part].wait_recv()
                arrived = wide(row_in.at[half, a % RING, SIDE[1] + part]) + wide(
                    row_in.at[half, a % RING, SIDE[-1] + part]
                )
                row_kept[half, a % RING, pl.ds(part * part_rows, part_rows)] = (
                    mine[part * part_rows : (part + 1) * part_rows] + arrived
                )

    def send_swap(dx):
        slot = dx % RING
        out = col_swap_out.at[slot]
        out[...] = acc_ref[rows(here.col_piece(dx=dx, dcore=1) * piece, piece)].astype(jnp.bfloat16)
        col_swap[dx] = links.send(out, col_pair.at[slot], sibling)

    def core_start():
        for d in ROW_ORDER:
            chunk = lax.rem(row + d, row_count)
            stage["row", d] = links.send(
                core_out.at[rows(chunk * row_part, row_part)], core_in.at[d], row_device(d)
            )

    last_pass, last_in = {}, {}

    def last_out(half, slot, a, part):
        out = row_out.at[half, RING, slot]
        out[...] = row_kept[half, a % RING, pl.ds(part * part_rows, part_rows)].astype(jnp.bfloat16)
        return out

    def last_far():
        for half in halves:
            for sign in (1, -1):
                out = last_out(half, near(sign), 2, near(sign))
                last_pass[half, sign] = links.send(out, row_in.at[half, RING, PASS[sign]], first(half, sign))

    def last_plain(sign):
        for half in halves:
            part = 1 - near(sign)
            out = last_out(half, 2 + part, sign, part)
            last_in[half, sign, part] = links.send(
                out, row_in.at[half, RING, SIDE[sign] + part], first(half, sign)
            )

    def last_sum(sign):
        for half in halves:
            part = near(sign)
            last_pass[half, sign].wait_recv()
            total = row_kept[half, sign % RING, pl.ds(part * part_rows, part_rows)] + wide(
                row_in.at[half, RING, PASS[sign]]
            )
            out = row_out.at[half, RING, 4 + part]
            out[...] = total.astype(jnp.bfloat16)
            last_in[half, sign, part] = links.send(
                out, row_in.at[half, RING, SIDE[sign] + part], first(half, sign)
            )

    col_pass, col_side = {}, {}

    def col_sum(dx):
        mine = acc_ref[rows(here.col_piece(dx=dx) * piece, piece)]
        col_swap[dx].wait_recv()
        return mine + wide(col_pair.at[dx % RING])

    def half_of(part):
        return pl.ds(part * half_rows, half_rows)

    def col_far():
        col_out[0] = col_sum(2).astype(jnp.bfloat16)
        for sign in (1, -1):
            col_pass[sign] = links.send(
                col_out.at[0, half_of(near(sign))], col_in.at[PASS[sign]], here.device(dx=sign)
            )

    def col_plain(sign):
        total = col_sum(sign)
        slot = 1 if sign == 1 else 2
        part = near(sign)
        col_own[slot - 1] = total[part * half_rows : (part + 1) * half_rows]
        part = 1 - near(sign)
        col_out[slot, half_of(part)] = total[part * half_rows : (part + 1) * half_rows].astype(jnp.bfloat16)
        col_side[sign, part] = links.send(
            col_out.at[slot, half_of(part)], col_in.at[SIDE[sign] + part], here.device(dx=sign)
        )

    def col_pass_on(sign):
        slot = 1 if sign == 1 else 2
        part = near(sign)
        col_pass[sign].wait_recv()
        col_out[slot, half_of(part)] = (col_own[slot - 1] + wide(col_in.at[PASS[sign]])).astype(jnp.bfloat16)
        col_side[sign, part] = links.send(
            col_out.at[slot, half_of(part)], col_in.at[SIDE[sign] + part], here.device(dx=sign)
        )

    def col_close():
        total = col_sum(0)
        for part in (0, 1):
            for sign in (1, -1):
                col_side[sign, part].wait_recv()
            grad_ref[half_of(part)] = (
                total[part * half_rows : (part + 1) * half_rows]
                + wide(col_in.at[SIDE[1] + part])
                + wide(col_in.at[SIDE[-1] + part])
            )

    def core_to_y():
        for d in range(1, row_count):
            stage["row", d].wait_recv()
        total = core_terms[rows(row * row_part, row_part)]
        for d in range(1, row_count):
            total += wide(core_in.at[d])
        core_y[here.y] = total.astype(jnp.bfloat16)
        for d in (2, 1, 3):
            stage["y", d] = links.send(core_y.at[here.y], core_y.at[here.y], here.device(dy=d))

    def core_to_z():
        for d in (1, 2, 3):
            stage["y", d].wait_recv()
        total = (wide(core_y.at[0]) + wide(core_y.at[1])) + (wide(core_y.at[2]) + wide(core_y.at[3]))
        core_z[here.z] = total.astype(jnp.bfloat16)
        for d in (2, 1, 3):
            stage["z", d] = links.send(core_z.at[here.z], core_z.at[here.z], here.device(dz=d))

    def core_back_row():
        for d in (1, 2, 3):
            stage["z", d].wait_recv()
        spot = core_all.at[rows(row * row_part, row_part)]
        spot[...] = (wide(core_z.at[0]) + wide(core_z.at[1])) + (wide(core_z.at[2]) + wide(core_z.at[3]))
        for d in (2, 1, 3):
            stage["bx", d] = links.send(spot, spot, row_device(2 * d))
        stage["chip", 0] = links.send(spot, spot, sibling)

    def core_back_chip():
        for d in (1, 3, 2):
            stage["bx", d].wait_recv()
            from_row = lax.rem(row + 2 * (RING - d), row_count)
            spot = core_all.at[rows(from_row * row_part, row_part)]
            stage["chip", d] = links.send(spot, spot, sibling)

    def core_close():
        for d in range(RING):
            stage["chip", d].wait_recv()
        core_total_ref[...] = core_all[...]

    core_start()
    send_far(2)
    send_far(1)
    send_far(-1)
    send_far(0)
    send_swap(2)
    send_swap(1)
    send_swap(-1)
    send_swap(0)
    send_plain(2)
    core_to_y()
    send_sum(2)
    send_plain(1)
    col_far()
    col_plain(1)
    col_plain(-1)
    send_sum(1)
    core_to_z()
    send_plain(-1)
    send_plain(0)
    close(2)
    last_far()
    core_back_row()
    send_sum(-1)
    send_sum(0)
    close(1)
    last_plain(1)
    core_back_chip()
    col_pass_on(1)
    col_pass_on(-1)
    close(-1)
    last_plain(-1)
    last_sum(1)
    last_sum(-1)
    col_close()
    links.drain(8)
    close(0)
    core_close()
    for half in halves:
        for part in (0, 1):
            for sign in (1, -1):
                last_in[half, sign, part].wait_recv()
            spot = pl.ds(half * half_rows + part * part_rows, part_rows)
            grad_ref[spot] += (
                row_kept[half, 0, pl.ds(part * part_rows, part_rows)]
                + wide(row_in.at[half, RING, SIDE[1] + part])
                + wide(row_in.at[half, RING, SIDE[-1] + part])
            )
    links.drain()


def reduce(shared, col_acc, turned, cores, piece):
    width = turned.shape[0]
    layers = cores.shape[0]
    half_rows, part_rows = piece // 2, piece // 4
    rank = width
    low, full = jnp.bfloat16, jnp.float32
    anywhere = pl.BlockSpec(memory_space=pl.ANY)
    inside = pl.BlockSpec(memory_space=pltpu.VMEM)
    return pl.pallas_call(
        reduce_kernel,
        out_shape=(
            jax.ShapeDtypeStruct((piece, width), full),
            jax.ShapeDtypeStruct((layers * rank, width), full),
        ),
        in_specs=[inside, inside, inside, anywhere],
        out_specs=(inside, inside),
        scratch_shapes=[
            pltpu.VMEM(cores.shape, full),
            pltpu.VMEM(cores.shape, low),
            pltpu.VMEM((layers * rank, width), full),
            pltpu.VMEM((2, RING + 1, 6, part_rows, width), low),
            pltpu.VMEM((2, RING + 1, 6, part_rows, width), low),
            pltpu.VMEM((2, RING, half_rows, width), full),
            pltpu.VMEM((RING, piece, width), low),
            pltpu.VMEM((2, half_rows, width), full),
            pltpu.VMEM((RING, piece, width), low),
            pltpu.VMEM((6, half_rows, width), low),
            pltpu.VMEM((3, piece, width), low),
            pltpu.VMEM((layers * rank, width), low),
            pltpu.VMEM((2 * RING, layers * rank // (2 * RING), width), low),
            pltpu.VMEM((RING, layers * rank // (2 * RING), width), low),
            pltpu.VMEM((RING, layers * rank // (2 * RING), width), low),
            pltpu.VMEM((layers * rank, width), full),
            pltpu.SemaphoreType.DMA((REDUCE_SENDS,)),
            pltpu.SemaphoreType.DMA((REDUCE_SENDS,)),
            pltpu.SemaphoreType.DMA((1,)),
        ],
        compiler_params=pltpu.CompilerParams(
            collective_id=1, has_side_effects=True, vmem_limit_bytes=18 * 1024 * 1024
        ),
        name="reduce_terms",
    )(shared, col_acc, turned, cores)


def on_device(factor, relation_cores, block_coords, block_values, block_counts):
    slot_count = block_values.shape[3]
    cells = lax.axis_size("row") * lax.axis_size("col")
    layers = relation_cores.shape[0]
    factor_far, cores_far = outside(factor), outside(relation_cores)
    turned, col_all, forward, shared, col_acc = map(pinned, gather(factor_far, cores_far))
    shared, col_acc = map(
        pinned,
        local_terms(
            outside(block_coords.reshape(layers * 2, slot_count)),
            outside(block_counts.reshape(layers)),
            forward,
            col_all,
            block_values,
            shared,
            col_acc,
        ),
    )
    gradient, core_total = reduce(shared, col_acc, turned, cores_far, factor.shape[0])
    factor_next = (factor.astype(jnp.float32) - step_factor * gradient).astype(jnp.bfloat16)
    core_total = core_total.reshape(relation_cores.shape) * (1.0 / factor.shape[1])
    cores_next = relation_cores - step_core / math.sqrt(cells * slot_count) * core_total
    return (factor_next, cores_next)


def solution(mesh):
    placed = (
        P(("row", "col"), None),
        P(),
        P(None, "row", "col", None, None),
        P(None, "row", "col", None, None, None),
        P(None, "row", "col"),
    )
    return jax.shard_map(
        on_device,
        mesh=mesh,
        in_specs=placed,
        out_specs=(P(("row", "col"), None), P()),
        check_vma=False,
    )
```

```python
import math

import jax
import jax.numpy as jnp
from jax import lax
from jax.experimental import pallas as pl
from jax.experimental.pallas import tpu as pltpu
from jax.sharding import PartitionSpec as P

step_factor = 0.25
step_core = 4.0

RING = 4
GROUP = 16
DEPTH = 3
MESH = pl.DeviceIdType.MESH


class Place:
    def __init__(self):
        row = lax.axis_index("row")
        col = lax.axis_index("col")
        self.x, self.core = lax.div(row, 2), lax.rem(row, 2)
        self.y, self.z = lax.div(col, RING), lax.rem(col, RING)

    def shifted(self, dx=0, dy=0, dz=0, dcore=0):
        x = lax.rem(self.x + dx + RING, RING)
        y = lax.rem(self.y + dy + RING, RING)
        z = lax.rem(self.z + dz + RING, RING)
        core = lax.rem(self.core + dcore, 2)
        return x, y, z, core

    def device(self, **shift):
        x, y, z, core = self.shifted(**shift)
        return (x * 2 + core, y * RING + z)

    def row_piece(self, **shift):
        _, y, z, _ = self.shifted(**shift)
        return y * RING + z

    def col_piece(self, **shift):
        x, _, _, core = self.shifted(**shift)
        return x * 2 + core


def dot_nn(left, right):
    return jnp.dot(left, right, preferred_element_type=jnp.float32)


def dot_nt(left, right):
    return lax.dot_general(left, right, (((1,), (1,)), ((), ())), preferred_element_type=jnp.float32)


def dot_tn(left, right):
    return lax.dot_general(left, right, (((0,), (0,)), ((), ())), preferred_element_type=jnp.float32)


def axes_of(half, a, b):
    return {"dy": a, "dz": b} if half == 0 else {"dy": b, "dz": a}


class Copies:
    def __init__(self, send_sems, recv_sems, local_sems):
        self.send_sems, self.recv_sems, self.local_sems = send_sems, recv_sems, local_sems
        self.sent, self.kept, self.drained = [], 0, 0

    def send(self, src, dst, device):
        number = len(self.sent)
        copy = pltpu.make_async_remote_copy(
            src_ref=src,
            dst_ref=dst,
            send_sem=self.send_sems.at[number],
            recv_sem=self.recv_sems.at[number],
            device_id=device,
            device_id_type=MESH,
        )
        copy.start()
        self.sent.append(copy)
        return copy

    def local(self, src, dst):
        copy = pltpu.make_async_copy(src, dst, self.local_sems.at[self.kept])
        self.kept += 1
        copy.start()
        return copy

    def drain(self, keep=0):
        last = len(self.sent) - keep
        for copy in self.sent[self.drained : last]:
            copy.wait_send()
        self.drained = max(self.drained, last)


def greet(devices, meanwhile=None):
    barrier = pltpu.get_barrier_semaphore()
    for device in devices:
        pl.semaphore_signal(barrier, inc=1, device_id=device, device_id_type=MESH)
    if meanwhile is not None:
        meanwhile()
    pl.semaphore_wait(barrier, len(devices))


def outside(x):
    return pltpu.with_memory_space_constraint(x, pltpu.HBM)


def pinned(x):
    return pltpu.with_memory_space_constraint(x, pltpu.VMEM)


def rows(start, size):
    return pl.ds(pl.multiple_of(start, 128 if size % 128 == 0 else 16), size)


GATHER_SENDS = 60 + 8


def gather_kernel(
    factor_ref,
    cores_ref,
    turned_ref,
    col_ref,
    forward_ref,
    shared_ref,
    acc_ref,
    row_ref,
    cores,
    low,
    send_sems,
    recv_sems,
    local_sems,
):
    here = Place()
    piece = factor_ref.shape[0]
    half_rows, part_rows = piece // 2, piece // 4
    total_rows = row_ref.shape[0]
    layers, rank, _ = cores_ref.shape
    links = Copies(send_sems, recv_sems, local_sems)
    cores_in = links.local(cores_ref, cores)
    greet(
        [here.device(dx=d) for d in (1, -1)]
        + [here.device(dy=d) for d in (1, -1)]
        + [here.device(dz=d) for d in (1, -1)]
        + [here.device(dcore=1)]
    )

    def region(half, a, b, part=None):
        start = here.row_piece(**axes_of(half, a, b)) * piece + half * half_rows
        if part is None:
            return row_ref.at[rows(start, half_rows)]
        return row_ref.at[rows(start + part * part_rows, part_rows)]

    def col_region(dx, dcore, half=None):
        start = here.col_piece(dx=dx, dcore=dcore) * piece
        if half is None:
            return col_ref.at[rows(start, piece)]
        return col_ref.at[rows(start + half * half_rows, half_rows)]

    def first(half, sign):
        return here.device(**axes_of(half, sign, 0))

    def second(half, sign):
        return here.device(**axes_of(half, 0, sign))

    halves = (0, 1)
    along, ahead, far, back, col_along, col_far = {}, {}, {}, {}, {}, {}
    sibling = here.device(dcore=1)
    across = []

    def near(sign):
        return 0 if sign == 1 else 1

    def own(half, part):
        return factor_ref.at[pl.ds(half * half_rows + part * part_rows, part_rows)]

    def send_along(passed):
        for half in halves:
            for sign in (1, -1):
                part = near(sign) if passed else 1 - near(sign)
                along[half, sign, part] = links.send(
                    own(half, part), region(half, 0, 0, part), first(half, sign)
                )

    def send_own(passed):
        for half in halves:
            for sign in (1, -1):
                part = near(sign) if passed else 1 - near(sign)
                ahead[half, 0, sign, part] = links.send(
                    own(half, part), region(half, 0, 0, part), second(half, sign)
                )

    def spread(half, a, part):
        spot = region(half, a, 0, part)
        for sign in (1, -1) if part == 0 else (-1, 1):
            ahead[half, a, sign, part] = links.send(spot, spot, second(half, sign))

    def take_along(passed):
        for sign in (1, -1):
            part = near(sign) if passed else 1 - near(sign)
            for half in halves:
                along[half, sign, part].wait_recv()
                if passed:
                    spot = region(half, -sign, 0, part)
                    far[half, sign] = links.send(spot, spot, first(half, sign))
                spread(half, -sign, part)

    def take_far():
        for sign in (1, -1):
            for half in halves:
                far[half, sign].wait_recv()
                spread(half, 2, near(sign))

    def pass_on(a):
        for half in halves:
            for sign in (1, -1):
                part = near(sign)
                ahead[half, a, sign, part].wait_recv()
                spot = region(half, a, -sign, part)
                back[half, a, sign] = links.send(spot, spot, second(half, sign))

    def take_rest(a):
        for half in halves:
            for sign in (1, -1):
                ahead[half, a, sign, 1 - near(sign)].wait_recv()

    def take_back(a):
        for half in halves:
            for sign in (1, -1):
                back[half, a, sign].wait_recv()

    def widen(half, a, b):
        start = here.row_piece(**axes_of(half, a, b)) * piece + half * half_rows
        arrived = row_ref[rows(start, half_rows)]
        turned_ref[:, rows(start, half_rows)] = arrived.T
        product = dot_nn(arrived, low[...]) * (1.0 / rank)
        for layer in range(layers):
            forward_ref[rows(layer * total_rows + start, half_rows)] = product[
                :, layer * rank : (layer + 1) * rank
            ].astype(jnp.bfloat16)

    def widen_all(a, b):
        for half in halves:
            widen(half, a, b)

    def col_start():
        for sign in (1, -1):
            col_along[sign] = links.send(factor_ref, col_region(0, 0), here.device(dx=sign))
        across.append(links.send(factor_ref, col_region(0, 0), sibling))

    def col_pass():
        for sign in (1, -1):
            col_along[sign].wait_recv()
            spot = col_region(-sign, 0, near(sign))
            col_far[sign] = links.send(spot, spot, here.device(dx=sign))
            across.append(links.send(col_region(-sign, 0), col_region(-sign, 0), sibling))

    def col_end():
        for sign in (1, -1):
            col_far[sign].wait_recv()
        across.append(links.send(col_region(2, 0), col_region(2, 0), sibling))

    def prepare():
        zero_rows = 512

        @pl.loop(0, shared_ref.shape[0] // zero_rows)
        def _(index):
            shared_ref[rows(index * zero_rows, zero_rows)] = jnp.zeros((zero_rows, rank), jnp.float32)

        @pl.loop(0, acc_ref.shape[0] // zero_rows)
        def _(index):
            acc_ref[rows(index * zero_rows, zero_rows)] = jnp.zeros((zero_rows, rank), jnp.float32)

        cores_in.wait()
        for layer in range(layers):
            low[:, layer * rank : (layer + 1) * rank] = cores[layer].astype(jnp.bfloat16)
        for copy in kept:
            copy.wait()

    def drain():
        links.drain(4)

    def finish():
        for copy in across:
            copy.wait_recv()
        links.drain()

    kept = [
        links.local(factor_ref, row_ref.at[rows(here.row_piece() * piece, piece)]),
        links.local(factor_ref, col_region(0, 0)),
    ]
    send_along(True)
    send_along(False)
    send_own(True)
    send_own(False)
    col_start()
    prepare()
    widen_all(0,0)
    take_along(True)
    take_along(False)
    widen_all(-1,0)
    widen_all(1,0)
    col_pass()
    take_far()
    pass_on(0)
    widen_all(2,0)
    col_end()
    take_rest(0)
    widen_all(0,1)
    widen_all(0,-1)
    pass_on(-1)
    take_rest(-1)
    widen_all(-1,1)
    widen_all(-1,-1)
    pass_on(1)
    take_rest(1)
    widen_all(1,1)
    widen_all(1,-1)
    pass_on(2)
    take_rest(2)
    widen_all(2,1)
    widen_all(2,-1)
    take_back(0)
    widen_all(0,2)
    take_back(-1)
    widen_all(-1,2)
    take_back(1)
    widen_all(1,2)
    drain()
    take_back(2)
    widen_all(2,2)
    finish()

def gather(factor, cores):
    piece, width = factor.shape
    layers = cores.shape[0]
    row_shape, col_shape = (RING * RING * piece, width), (RING * 2 * piece, width)
    wide_shape = (layers * row_shape[0], width)
    anywhere, inside = pl.BlockSpec(memory_space=pl.ANY), pl.BlockSpec(memory_space=pltpu.VMEM)
    return pl.pallas_call(
        gather_kernel,
        out_shape=(
            pltpu.VMEM(row_shape[::-1], factor.dtype),
            pltpu.VMEM(col_shape, factor.dtype),
            pltpu.VMEM(wide_shape, jnp.bfloat16),
            pltpu.VMEM(wide_shape, jnp.float32),
            pltpu.VMEM(col_shape, jnp.float32),
        ),
        in_specs=[anywhere, anywhere],
        out_specs=(inside,) * 5,
        scratch_shapes=[
            pltpu.VMEM(row_shape, factor.dtype),
            pltpu.VMEM(cores.shape, jnp.float32),
            pltpu.VMEM((width, layers * width), jnp.bfloat16),
            pltpu.SemaphoreType.DMA((GATHER_SENDS,)),
            pltpu.SemaphoreType.DMA((GATHER_SENDS,)),
            pltpu.SemaphoreType.DMA((3,)),
        ],
        compiler_params=pltpu.CompilerParams(
            collective_id=0, has_side_effects=True, vmem_limit_bytes=8 * 1024 * 1024
        ),
        name="gather_factor",
    )(factor, cores)


def block_kernel(
    coords_hbm,
    counts_hbm,
    forward,
    col_all,
    values_hbm,
    shared_in,
    acc_in,
    shared,
    col_acc,
    values,
    coords_ref,
    counts_ref,
    value_sems,
    scalar_sems,
):
    layers, block = 2, values.shape[-1]
    total_rows = forward.shape[0] // layers
    coords_in = pltpu.make_async_copy(coords_hbm, coords_ref, scalar_sems.at[0])
    counts_in = pltpu.make_async_copy(counts_hbm, counts_ref, scalar_sems.at[1])
    first_values = pltpu.make_async_copy(values_hbm.at[0, 0, 0, pl.ds(0, GROUP)], values.at[0], value_sems.at[0])
    counts_in.start()
    coords_in.start()
    first_values.start()
    counts_in.wait()
    groups = [(counts_ref[layer] + GROUP - 1) // GROUP for layer in range(layers)]
    total = groups[0] + groups[1]

    def slot_of(step):
        layer = (step >= groups[0]).astype(jnp.int32)
        return layer, (step - layer * groups[0]) * GROUP

    def value_load(step):
        layer, first_slot = slot_of(step)
        place = lax.rem(step, DEPTH)
        return pltpu.make_async_copy(
            values_hbm.at[layer, 0, 0, pl.ds(first_slot, GROUP)], values.at[place], value_sems.at[place]
        )

    for step in range(1, DEPTH - 1):

        @pl.when(step < total)
        def _():
            value_load(jnp.int32(step)).start()

    coords_in.wait()

    @pl.loop(0, total)
    def _(step):
        value_load(step).wait()

        @pl.when(step + DEPTH - 1 < total)
        def _():
            value_load(step + DEPTH - 1).start()

        layer, first_slot = slot_of(step)
        place = lax.rem(step, DEPTH)
        spots = []
        for slot in range(GROUP):
            row_block = coords_ref[layer * 2, first_slot + slot]
            col_block = coords_ref[layer * 2 + 1, first_slot + slot]
            row_start = pl.multiple_of(layer * total_rows + row_block * block, block)
            col_start = pl.multiple_of(col_block * block, block)
            spots.append((pl.ds(row_start, block), pl.ds(col_start, block)))
        residuals = []
        for slot in range(GROUP):
            row_spot, col_spot = spots[slot]
            predicted = dot_nt(forward[row_spot], col_all[col_spot])
            live = first_slot + slot < counts_ref[layer]
            residual = jnp.where(live, predicted - values[place, slot].astype(jnp.float32), 0.0)
            residuals.append(residual.astype(jnp.bfloat16))
        for slot in range(GROUP):
            row_spot, col_spot = spots[slot]
            shared[row_spot] += dot_nn(residuals[slot], col_all[col_spot])
            col_acc[col_spot] += dot_tn(residuals[slot], forward[row_spot])


def local_terms(coords, counts, forward, col_all, block_values, shared, col_acc):
    block = block_values.shape[-1]
    scalars, inside = pl.BlockSpec(memory_space=pl.ANY), pl.BlockSpec(memory_space=pltpu.VMEM)
    return pl.pallas_call(
        block_kernel,
        out_shape=(pltpu.VMEM(shared.shape, jnp.float32), pltpu.VMEM(col_acc.shape, jnp.float32)),
        in_specs=[scalars, scalars, inside, inside, pl.BlockSpec(memory_space=pl.ANY), inside, inside],
        out_specs=(inside, inside),
        input_output_aliases={5: 0, 6: 1},
        scratch_shapes=[
            pltpu.VMEM((DEPTH, GROUP, block, block), jnp.int32),
            pltpu.SMEM(coords.shape, jnp.int32),
            pltpu.SMEM(counts.shape, jnp.int32),
            pltpu.SemaphoreType.DMA((DEPTH,)),
            pltpu.SemaphoreType.DMA((2,)),
        ],
        compiler_params=pltpu.CompilerParams(vmem_limit_bytes=12 * 1024 * 1024),
        name="block_terms",
    )(coords, counts, forward, col_all, block_values, shared, col_acc)


REDUCE_SENDS = 60 + 10 + 20
ROW_ORDER = (4, 5, 3, 2, 6, 7, 1)
PASS, SIDE = {1: 0, -1: 1}, {1: 2, -1: 4}


def reduce_kernel(
    shared_ref,
    acc_ref,
    turned_ref,
    cores_ref,
    grad_ref,
    core_total_ref,
    cores,
    low,
    core_terms,
    row_in,
    row_out,
    row_kept,
    col_swap_out,
    col_own,
    col_pair,
    col_in,
    col_out,
    core_out,
    core_in,
    core_y,
    core_z,
    core_all,
    send_sems,
    recv_sems,
    local_sems,
):
    here = Place()
    piece, width = grad_ref.shape
    half_rows, part_rows = piece // 2, piece // 4
    total_rows = turned_ref.shape[1]
    layers, rank, _ = cores_ref.shape
    links = Copies(send_sems, recv_sems, local_sems)
    cores_in = links.local(cores_ref, cores)
    row_count = 2 * RING
    row, col = lax.axis_index("row"), lax.axis_index("col")

    def row_device(d):
        return (lax.rem(row + d, row_count), col)

    partners = [row_device(d) for d in range(1, row_count)]
    partners += [here.device(**{"d" + axis: d}) for axis in "yz" for d in (1, 2, 3)]
    row_part = layers * rank // row_count

    def core_terms_here():
        core_terms[...] = jnp.zeros_like(core_terms)
        step_rows = 8192

        @pl.loop(0, total_rows // step_rows)
        def _(index):
            start = index * step_rows
            own = turned_ref[:, rows(start, step_rows)]
            for layer in range(layers):
                sums = shared_ref[rows(layer * total_rows + start, step_rows)].astype(jnp.bfloat16)
                core_terms[pl.ds(layer * rank, rank)] += dot_nn(own, sums)

        core_out[...] = core_terms[...].astype(jnp.bfloat16)

    greet(partners, core_terms_here)
    halves = (0, 1)
    cores_in.wait()
    for layer in range(layers):
        low[layer] = cores[layer].astype(jnp.bfloat16)

    def term(half, a, b):
        start = here.row_piece(**axes_of(half, a, b)) * piece + half * half_rows
        total = None
        for layer in range(layers):
            sums = shared_ref[rows(layer * total_rows + start, half_rows)].astype(jnp.bfloat16)
            product = dot_nt(sums, low[layer])
            total = product if total is None else total + product
        return total * (1.0 / rank)

    def first(half, sign):
        return here.device(**axes_of(half, sign, 0))

    def second(half, sign):
        return here.device(**axes_of(half, 0, sign))

    def wide(ref):
        return ref[...].astype(jnp.float32)

    def quarter(part):
        return pl.ds(part * part_rows, part_rows)

    def near(sign):
        return 0 if sign == 1 else 1

    sibling = here.device(dcore=1)
    pass_in, side_in, col_swap, stage = {}, {}, {}, {}

    def send_far(a):
        for half in halves:
            both = term(half, a, 2).astype(jnp.bfloat16)
            for sign in (1, -1):
                part = near(sign)
                out = row_out.at[half, a % RING, PASS[sign]]
                out[...] = both[part * part_rows : (part + 1) * part_rows]
                pass_in[half, a, sign] = links.send(
                    out, row_in.at[half, a % RING, PASS[sign]], second(half, sign)
                )

    def send_plain(a):
        for half in halves:
            for sign in (1, -1):
                part = 1 - near(sign)
                both = term(half, a, sign)
                out = row_out.at[half, a % RING, SIDE[sign] + part]
                out[...] = both[part * part_rows : (part + 1) * part_rows].astype(jnp.bfloat16)
                row_kept[half, a % RING, quarter(1 - part)] = both[
                    (1 - part) * part_rows : (2 - part) * part_rows
                ]
                side_in[half, a, sign, part] = links.send(
                    out, row_in.at[half, a % RING, SIDE[sign] + part], second(half, sign)
                )

    def send_sum(a):
        for half in halves:
            for sign in (1, -1):
                part = near(sign)
                mine = row_kept[half, a % RING, quarter(part)]
                pass_in[half, a, sign].wait_recv()
                arrived = wide(row_in.at[half, a % RING, PASS[sign]])
                out = row_out.at[half, a % RING, SIDE[sign] + part]
                out[...] = (mine + arrived).astype(jnp.bfloat16)
                side_in[half, a, sign, part] = links.send(
                    out, row_in.at[half, a % RING, SIDE[sign] + part], second(half, sign)
                )

    def close(a):
        for half in halves:
            mine = term(half, a, 0)
            for part in (0, 1):
                for sign in (1, -1):
                    side_in[half, a, sign, part].wait_recv()
                arrived = wide(row_in.at[half, a % RING, SIDE[1] + part]) + wide(
                    row_in.at[half, a % RING, SIDE[-1] + part]
                )
                row_kept[half, a % RING, pl.ds(part * part_rows, part_rows)] = (
                    mine[part * part_rows : (part + 1) * part_rows] + arrived
                )

    def send_swap(dx):
        slot = dx % RING
        out = col_swap_out.at[slot]
        out[...] = acc_ref[rows(here.col_piece(dx=dx, dcore=1) * piece, piece)].astype(jnp.bfloat16)
        col_swap[dx] = links.send(out, col_pair.at[slot], sibling)

    def core_start():
        for d in ROW_ORDER:
            chunk = lax.rem(row + d, row_count)
            stage["row", d] = links.send(
                core_out.at[rows(chunk * row_part, row_part)], core_in.at[d], row_device(d)
            )

    last_pass, last_in = {}, {}

    def last_out(half, slot, a, part):
        out = row_out.at[half, RING, slot]
        out[...] = row_kept[half, a % RING, pl.ds(part * part_rows, part_rows)].astype(jnp.bfloat16)
        return out

    def last_far():
        for half in halves:
            for sign in (1, -1):
                out = last_out(half, near(sign), 2, near(sign))
                last_pass[half, sign] = links.send(out, row_in.at[half, RING, PASS[sign]], first(half, sign))

    def last_plain(sign):
        for half in halves:
            part = 1 - near(sign)
            out = last_out(half, 2 + part, sign, part)
            last_in[half, sign, part] = links.send(
                out, row_in.at[half, RING, SIDE[sign] + part], first(half, sign)
            )

    def last_sum(sign):
        for half in halves:
            part = near(sign)
            last_pass[half, sign].wait_recv()
            total = row_kept[half, sign % RING, pl.ds(part * part_rows, part_rows)] + wide(
                row_in.at[half, RING, PASS[sign]]
            )
            out = row_out.at[half, RING, 4 + part]
            out[...] = total.astype(jnp.bfloat16)
            last_in[half, sign, part] = links.send(
                out, row_in.at[half, RING, SIDE[sign] + part], first(half, sign)
            )

    col_pass, col_side = {}, {}

    def col_sum(dx):
        mine = acc_ref[rows(here.col_piece(dx=dx) * piece, piece)]
        col_swap[dx].wait_recv()
        return mine + wide(col_pair.at[dx % RING])

    def half_of(part):
        return pl.ds(part * half_rows, half_rows)

    def col_far():
        col_out[0] = col_sum(2).astype(jnp.bfloat16)
        for sign in (1, -1):
            col_pass[sign] = links.send(
                col_out.at[0, half_of(near(sign))], col_in.at[PASS[sign]], here.device(dx=sign)
            )

    def col_plain(sign):
        total = col_sum(sign)
        slot = 1 if sign == 1 else 2
        part = near(sign)
        col_own[slot - 1] = total[part * half_rows : (part + 1) * half_rows]
        part = 1 - near(sign)
        col_out[slot, half_of(part)] = total[part * half_rows : (part + 1) * half_rows].astype(jnp.bfloat16)
        col_side[sign, part] = links.send(
            col_out.at[slot, half_of(part)], col_in.at[SIDE[sign] + part], here.device(dx=sign)
        )

    def col_pass_on(sign):
        slot = 1 if sign == 1 else 2
        part = near(sign)
        col_pass[sign].wait_recv()
        col_out[slot, half_of(part)] = (col_own[slot - 1] + wide(col_in.at[PASS[sign]])).astype(jnp.bfloat16)
        col_side[sign, part] = links.send(
            col_out.at[slot, half_of(part)], col_in.at[SIDE[sign] + part], here.device(dx=sign)
        )

    def col_close():
        total = col_sum(0)
        for part in (0, 1):
            for sign in (1, -1):
                col_side[sign, part].wait_recv()
            grad_ref[half_of(part)] = (
                total[part * half_rows : (part + 1) * half_rows]
                + wide(col_in.at[SIDE[1] + part])
                + wide(col_in.at[SIDE[-1] + part])
            )

    def core_to_y():
        for d in range(1, row_count):
            stage["row", d].wait_recv()
        total = core_terms[rows(row * row_part, row_part)]
        for d in range(1, row_count):
            total += wide(core_in.at[d])
        core_y[here.y] = total.astype(jnp.bfloat16)
        for d in (2, 1, 3):
            stage["y", d] = links.send(core_y.at[here.y], core_y.at[here.y], here.device(dy=d))

    def core_to_z():
        for d in (1, 2, 3):
            stage["y", d].wait_recv()
        total = (wide(core_y.at[0]) + wide(core_y.at[1])) + (wide(core_y.at[2]) + wide(core_y.at[3]))
        core_z[here.z] = total.astype(jnp.bfloat16)
        for d in (2, 1, 3):
            stage["z", d] = links.send(core_z.at[here.z], core_z.at[here.z], here.device(dz=d))

    def core_back_row():
        for d in (1, 2, 3):
            stage["z", d].wait_recv()
        spot = core_all.at[rows(row * row_part, row_part)]
        spot[...] = (wide(core_z.at[0]) + wide(core_z.at[1])) + (wide(core_z.at[2]) + wide(core_z.at[3]))
        for d in (2, 1, 3):
            stage["bx", d] = links.send(spot, spot, row_device(2 * d))
        stage["chip", 0] = links.send(spot, spot, sibling)

    def core_back_chip():
        for d in (1, 3, 2):
            stage["bx", d].wait_recv()
            from_row = lax.rem(row + 2 * (RING - d), row_count)
            spot = core_all.at[rows(from_row * row_part, row_part)]
            stage["chip", d] = links.send(spot, spot, sibling)

    def core_close():
        for d in range(RING):
            stage["chip", d].wait_recv()
        core_total_ref[...] = core_all[...]

    core_start()
    send_far(2)
    send_far(1)
    send_far(-1)
    send_far(0)
    send_swap(2)
    send_swap(1)
    send_swap(-1)
    send_swap(0)
    core_to_y()
    send_plain(2)
    send_sum(2)
    send_plain(1)
    core_to_z()
    col_far()
    col_plain(1)
    col_plain(-1)
    send_sum(1)
    send_plain(-1)
    send_plain(0)
    close(2)
    last_far()
    core_back_row()
    send_sum(-1)
    send_sum(0)
    core_back_chip()
    close(1)
    last_plain(1)
    col_pass_on(1)
    col_pass_on(-1)
    close(-1)
    last_plain(-1)
    last_sum(1)
    last_sum(-1)
    col_close()
    links.drain(8)
    core_close()
    close(0)
    for half in halves:
        for part in (0, 1):
            for sign in (1, -1):
                last_in[half, sign, part].wait_recv()
            spot = pl.ds(half * half_rows + part * part_rows, part_rows)
            grad_ref[spot] += (
                row_kept[half, 0, pl.ds(part * part_rows, part_rows)]
                + wide(row_in.at[half, RING, SIDE[1] + part])
                + wide(row_in.at[half, RING, SIDE[-1] + part])
            )
    links.drain()


def reduce(shared, col_acc, turned, cores, piece):
    width = turned.shape[0]
    layers = cores.shape[0]
    half_rows, part_rows = piece // 2, piece // 4
    rank = width
    low, full = jnp.bfloat16, jnp.float32
    anywhere = pl.BlockSpec(memory_space=pl.ANY)
    inside = pl.BlockSpec(memory_space=pltpu.VMEM)
    return pl.pallas_call(
        reduce_kernel,
        out_shape=(
            jax.ShapeDtypeStruct((piece, width), full),
            jax.ShapeDtypeStruct((layers * rank, width), full),
        ),
        in_specs=[inside, inside, inside, anywhere],
        out_specs=(inside, inside),
        scratch_shapes=[
            pltpu.VMEM(cores.shape, full),
            pltpu.VMEM(cores.shape, low),
            pltpu.VMEM((layers * rank, width), full),
            pltpu.VMEM((2, RING + 1, 6, part_rows, width), low),
            pltpu.VMEM((2, RING + 1, 6, part_rows, width), low),
            pltpu.VMEM((2, RING, half_rows, width), full),
            pltpu.VMEM((RING, piece, width), low),
            pltpu.VMEM((2, half_rows, width), full),
            pltpu.VMEM((RING, piece, width), low),
            pltpu.VMEM((6, half_rows, width), low),
            pltpu.VMEM((3, piece, width), low),
            pltpu.VMEM((layers * rank, width), low),
            pltpu.VMEM((2 * RING, layers * rank // (2 * RING), width), low),
            pltpu.VMEM((RING, layers * rank // (2 * RING), width), low),
            pltpu.VMEM((RING, layers * rank // (2 * RING), width), low),
            pltpu.VMEM((layers * rank, width), full),
            pltpu.SemaphoreType.DMA((REDUCE_SENDS,)),
            pltpu.SemaphoreType.DMA((REDUCE_SENDS,)),
            pltpu.SemaphoreType.DMA((1,)),
        ],
        compiler_params=pltpu.CompilerParams(
            collective_id=1, has_side_effects=True, vmem_limit_bytes=18 * 1024 * 1024
        ),
        name="reduce_terms",
    )(shared, col_acc, turned, cores)


def on_device(factor, relation_cores, block_coords, block_values, block_counts):
    slot_count = block_values.shape[3]
    cells = lax.axis_size("row") * lax.axis_size("col")
    layers = relation_cores.shape[0]
    factor_far, cores_far = outside(factor), outside(relation_cores)
    turned, col_all, forward, shared, col_acc = map(pinned, gather(factor_far, cores_far))
    shared, col_acc = map(
        pinned,
        local_terms(
            outside(block_coords.reshape(layers * 2, slot_count)),
            outside(block_counts.reshape(layers)),
            forward,
            col_all,
            block_values,
            shared,
            col_acc,
        ),
    )
    gradient, core_total = reduce(shared, col_acc, turned, cores_far, factor.shape[0])
    factor_next = (factor.astype(jnp.float32) - step_factor * gradient).astype(jnp.bfloat16)
    core_total = core_total.reshape(relation_cores.shape) * (1.0 / factor.shape[1])
    cores_next = relation_cores - step_core / math.sqrt(cells * slot_count) * core_total
    return (factor_next, cores_next)


def solution(mesh):
    placed = (
        P(("row", "col"), None),
        P(),
        P(None, "row", "col", None, None),
        P(None, "row", "col", None, None, None),
        P(None, "row", "col"),
    )
    return jax.shard_map(
        on_device,
        mesh=mesh,
        in_specs=placed,
        out_specs=(P(("row", "col"), None), P()),
        check_vma=False,
    )
```

```python
import math

import jax
import jax.numpy as jnp
from jax import lax
from jax.experimental import pallas as pl
from jax.experimental.pallas import tpu as pltpu
from jax.sharding import PartitionSpec as P

step_factor = 0.25
step_core = 4.0

RING = 4
GROUP = 16
DEPTH = 3
MESH = pl.DeviceIdType.MESH


class Place:
    def __init__(self):
        row = lax.axis_index("row")
        col = lax.axis_index("col")
        self.x, self.core = lax.div(row, 2), lax.rem(row, 2)
        self.y, self.z = lax.div(col, RING), lax.rem(col, RING)

    def shifted(self, dx=0, dy=0, dz=0, dcore=0):
        x = lax.rem(self.x + dx + RING, RING)
        y = lax.rem(self.y + dy + RING, RING)
        z = lax.rem(self.z + dz + RING, RING)
        core = lax.rem(self.core + dcore, 2)
        return x, y, z, core

    def device(self, **shift):
        x, y, z, core = self.shifted(**shift)
        return (x * 2 + core, y * RING + z)

    def row_piece(self, **shift):
        _, y, z, _ = self.shifted(**shift)
        return y * RING + z

    def col_piece(self, **shift):
        x, _, _, core = self.shifted(**shift)
        return x * 2 + core


def dot_nn(left, right):
    return jnp.dot(left, right, preferred_element_type=jnp.float32)


def dot_nt(left, right):
    return lax.dot_general(left, right, (((1,), (1,)), ((), ())), preferred_element_type=jnp.float32)


def dot_tn(left, right):
    return lax.dot_general(left, right, (((0,), (0,)), ((), ())), preferred_element_type=jnp.float32)


def axes_of(half, a, b):
    return {"dy": a, "dz": b} if half == 0 else {"dy": b, "dz": a}


class Copies:
    def __init__(self, send_sems, recv_sems, local_sems):
        self.send_sems, self.recv_sems, self.local_sems = send_sems, recv_sems, local_sems
        self.sent, self.kept, self.drained = [], 0, 0

    def send(self, src, dst, device):
        number = len(self.sent)
        copy = pltpu.make_async_remote_copy(
            src_ref=src,
            dst_ref=dst,
            send_sem=self.send_sems.at[number],
            recv_sem=self.recv_sems.at[number],
            device_id=device,
            device_id_type=MESH,
        )
        copy.start()
        self.sent.append(copy)
        return copy

    def local(self, src, dst):
        copy = pltpu.make_async_copy(src, dst, self.local_sems.at[self.kept])
        self.kept += 1
        copy.start()
        return copy

    def drain(self, keep=0):
        last = len(self.sent) - keep
        for copy in self.sent[self.drained : last]:
            copy.wait_send()
        self.drained = max(self.drained, last)


def greet(devices, meanwhile=None):
    barrier = pltpu.get_barrier_semaphore()
    for device in devices:
        pl.semaphore_signal(barrier, inc=1, device_id=device, device_id_type=MESH)
    if meanwhile is not None:
        meanwhile()
    pl.semaphore_wait(barrier, len(devices))


def outside(x):
    return pltpu.with_memory_space_constraint(x, pltpu.HBM)


def pinned(x):
    return pltpu.with_memory_space_constraint(x, pltpu.VMEM)


def rows(start, size):
    return pl.ds(pl.multiple_of(start, 128 if size % 128 == 0 else 16), size)


GATHER_SENDS = 60 + 8


def gather_kernel(
    factor_ref,
    cores_ref,
    turned_ref,
    col_ref,
    forward_ref,
    shared_ref,
    acc_ref,
    row_ref,
    cores,
    low,
    send_sems,
    recv_sems,
    local_sems,
):
    here = Place()
    piece = factor_ref.shape[0]
    half_rows, part_rows = piece // 2, piece // 4
    total_rows = row_ref.shape[0]
    layers, rank, _ = cores_ref.shape
    links = Copies(send_sems, recv_sems, local_sems)
    cores_in = links.local(cores_ref, cores)
    greet(
        [here.device(dx=d) for d in (1, -1)]
        + [here.device(dy=d) for d in (1, -1)]
        + [here.device(dz=d) for d in (1, -1)]
        + [here.device(dcore=1)]
    )

    def region(half, a, b, part=None):
        start = here.row_piece(**axes_of(half, a, b)) * piece + half * half_rows
        if part is None:
            return row_ref.at[rows(start, half_rows)]
        return row_ref.at[rows(start + part * part_rows, part_rows)]

    def col_region(dx, dcore, half=None):
        start = here.col_piece(dx=dx, dcore=dcore) * piece
        if half is None:
            return col_ref.at[rows(start, piece)]
        return col_ref.at[rows(start + half * half_rows, half_rows)]

    def first(half, sign):
        return here.device(**axes_of(half, sign, 0))

    def second(half, sign):
        return here.device(**axes_of(half, 0, sign))

    halves = (0, 1)
    along, ahead, far, back, col_along, col_far = {}, {}, {}, {}, {}, {}
    sibling = here.device(dcore=1)
    across = []

    def near(sign):
        return 0 if sign == 1 else 1

    def own(half, part):
        return factor_ref.at[pl.ds(half * half_rows + part * part_rows, part_rows)]

    def send_along(passed):
        for half in halves:
            for sign in (1, -1):
                part = near(sign) if passed else 1 - near(sign)
                along[half, sign, part] = links.send(
                    own(half, part), region(half, 0, 0, part), first(half, sign)
                )

    def send_own(passed):
        for half in halves:
            for sign in (1, -1):
                part = near(sign) if passed else 1 - near(sign)
                ahead[half, 0, sign, part] = links.send(
                    own(half, part), region(half, 0, 0, part), second(half, sign)
                )

    def spread(half, a, part):
        spot = region(half, a, 0, part)
        for sign in (1, -1) if part == 0 else (-1, 1):
            ahead[half, a, sign, part] = links.send(spot, spot, second(half, sign))

    def take_along(passed):
        for sign in (1, -1):
            part = near(sign) if passed else 1 - near(sign)
            for half in halves:
                along[half, sign, part].wait_recv()
                if passed:
                    spot = region(half, -sign, 0, part)
                    far[half, sign] = links.send(spot, spot, first(half, sign))
                spread(half, -sign, part)

    def take_far():
        for sign in (1, -1):
            for half in halves:
                far[half, sign].wait_recv()
                spread(half, 2, near(sign))

    def pass_on(a):
        for half in halves:
            for sign in (1, -1):
                part = near(sign)
                ahead[half, a, sign, part].wait_recv()
                spot = region(half, a, -sign, part)
                back[half, a, sign] = links.send(spot, spot, second(half, sign))

    def take_rest(a):
        for half in halves:
            for sign in (1, -1):
                ahead[half, a, sign, 1 - near(sign)].wait_recv()

    def take_back(a):
        for half in halves:
            for sign in (1, -1):
                back[half, a, sign].wait_recv()

    def widen(half, a, b):
        start = here.row_piece(**axes_of(half, a, b)) * piece + half * half_rows
        arrived = row_ref[rows(start, half_rows)]
        turned_ref[:, rows(start, half_rows)] = arrived.T
        product = dot_nn(arrived, low[...]) * (1.0 / rank)
        for layer in range(layers):
            forward_ref[rows(layer * total_rows + start, half_rows)] = product[
                :, layer * rank : (layer + 1) * rank
            ].astype(jnp.bfloat16)

    def widen_all(a, b):
        for half in halves:
            widen(half, a, b)

    def col_start():
        for sign in (1, -1):
            col_along[sign] = links.send(factor_ref, col_region(0, 0), here.device(dx=sign))
        across.append(links.send(factor_ref, col_region(0, 0), sibling))

    def col_pass():
        for sign in (1, -1):
            col_along[sign].wait_recv()
            spot = col_region(-sign, 0, near(sign))
            col_far[sign] = links.send(spot, spot, here.device(dx=sign))
            across.append(links.send(col_region(-sign, 0), col_region(-sign, 0), sibling))

    def col_end():
        for sign in (1, -1):
            col_far[sign].wait_recv()
        across.append(links.send(col_region(2, 0), col_region(2, 0), sibling))

    def prepare():
        zero_rows = 512

        @pl.loop(0, shared_ref.shape[0] // zero_rows)
        def _(index):
            shared_ref[rows(index * zero_rows, zero_rows)] = jnp.zeros((zero_rows, rank), jnp.float32)

        @pl.loop(0, acc_ref.shape[0] // zero_rows)
        def _(index):
            acc_ref[rows(index * zero_rows, zero_rows)] = jnp.zeros((zero_rows, rank), jnp.float32)

        cores_in.wait()
        for layer in range(layers):
            low[:, layer * rank : (layer + 1) * rank] = cores[layer].astype(jnp.bfloat16)
        for copy in kept:
            copy.wait()

    def drain():
        links.drain(4)

    def finish():
        for copy in across:
            copy.wait_recv()
        links.drain()

    kept = [
        links.local(factor_ref, row_ref.at[rows(here.row_piece() * piece, piece)]),
        links.local(factor_ref, col_region(0, 0)),
    ]
    send_along(True)
    send_along(False)
    send_own(True)
    send_own(False)
    col_start()
    prepare()
    widen_all(0,0)
    take_along(True)
    take_along(False)
    widen_all(-1,0)
    widen_all(1,0)
    col_pass()
    take_far()
    pass_on(0)
    widen_all(2,0)
    col_end()
    take_rest(0)
    widen_all(0,1)
    widen_all(0,-1)
    pass_on(-1)
    take_rest(-1)
    widen_all(-1,1)
    widen_all(-1,-1)
    pass_on(1)
    take_rest(1)
    widen_all(1,1)
    widen_all(1,-1)
    pass_on(2)
    take_rest(2)
    widen_all(2,1)
    widen_all(2,-1)
    take_back(0)
    widen_all(0,2)
    take_back(-1)
    widen_all(-1,2)
    take_back(1)
    widen_all(1,2)
    drain()
    take_back(2)
    widen_all(2,2)
    finish()

def gather(factor, cores):
    piece, width = factor.shape
    layers = cores.shape[0]
    row_shape, col_shape = (RING * RING * piece, width), (RING * 2 * piece, width)
    wide_shape = (layers * row_shape[0], width)
    anywhere, inside = pl.BlockSpec(memory_space=pl.ANY), pl.BlockSpec(memory_space=pltpu.VMEM)
    return pl.pallas_call(
        gather_kernel,
        out_shape=(
            pltpu.VMEM(row_shape[::-1], factor.dtype),
            pltpu.VMEM(col_shape, factor.dtype),
            pltpu.VMEM(wide_shape, jnp.bfloat16),
            pltpu.VMEM(wide_shape, jnp.float32),
            pltpu.VMEM(col_shape, jnp.float32),
        ),
        in_specs=[anywhere, anywhere],
        out_specs=(inside,) * 5,
        scratch_shapes=[
            pltpu.VMEM(row_shape, factor.dtype),
            pltpu.VMEM(cores.shape, jnp.float32),
            pltpu.VMEM((width, layers * width), jnp.bfloat16),
            pltpu.SemaphoreType.DMA((GATHER_SENDS,)),
            pltpu.SemaphoreType.DMA((GATHER_SENDS,)),
            pltpu.SemaphoreType.DMA((3,)),
        ],
        compiler_params=pltpu.CompilerParams(
            collective_id=0, has_side_effects=True, vmem_limit_bytes=8 * 1024 * 1024
        ),
        name="gather_factor",
    )(factor, cores)


def block_kernel(
    coords_hbm,
    counts_hbm,
    forward,
    col_all,
    values_hbm,
    shared_in,
    acc_in,
    shared,
    col_acc,
    values,
    coords_ref,
    counts_ref,
    value_sems,
    scalar_sems,
):
    layers, block = 2, values.shape[-1]
    total_rows = forward.shape[0] // layers
    coords_in = pltpu.make_async_copy(coords_hbm, coords_ref, scalar_sems.at[0])
    counts_in = pltpu.make_async_copy(counts_hbm, counts_ref, scalar_sems.at[1])
    first_values = pltpu.make_async_copy(values_hbm.at[0, 0, 0, pl.ds(0, GROUP)], values.at[0], value_sems.at[0])
    counts_in.start()
    coords_in.start()
    first_values.start()
    counts_in.wait()
    groups = [(counts_ref[layer] + GROUP - 1) // GROUP for layer in range(layers)]
    total = groups[0] + groups[1]

    def slot_of(step):
        layer = (step >= groups[0]).astype(jnp.int32)
        return layer, (step - layer * groups[0]) * GROUP

    def value_load(step):
        layer, first_slot = slot_of(step)
        place = lax.rem(step, DEPTH)
        return pltpu.make_async_copy(
            values_hbm.at[layer, 0, 0, pl.ds(first_slot, GROUP)], values.at[place], value_sems.at[place]
        )

    for step in range(1, DEPTH - 1):

        @pl.when(step < total)
        def _():
            value_load(jnp.int32(step)).start()

    coords_in.wait()

    @pl.loop(0, total)
    def _(step):
        value_load(step).wait()

        @pl.when(step + DEPTH - 1 < total)
        def _():
            value_load(step + DEPTH - 1).start()

        layer, first_slot = slot_of(step)
        place = lax.rem(step, DEPTH)
        spots = []
        for slot in range(GROUP):
            row_block = coords_ref[layer * 2, first_slot + slot]
            col_block = coords_ref[layer * 2 + 1, first_slot + slot]
            row_start = pl.multiple_of(layer * total_rows + row_block * block, block)
            col_start = pl.multiple_of(col_block * block, block)
            spots.append((pl.ds(row_start, block), pl.ds(col_start, block)))
        residuals = []
        for slot in range(GROUP):
            row_spot, col_spot = spots[slot]
            predicted = dot_nt(forward[row_spot], col_all[col_spot])
            live = first_slot + slot < counts_ref[layer]
            residual = jnp.where(live, predicted - values[place, slot].astype(jnp.float32), 0.0)
            residuals.append(residual.astype(jnp.bfloat16))
        for slot in range(GROUP):
            row_spot, col_spot = spots[slot]
            shared[row_spot] += dot_nn(residuals[slot], col_all[col_spot])
            col_acc[col_spot] += dot_tn(residuals[slot], forward[row_spot])


def local_terms(coords, counts, forward, col_all, block_values, shared, col_acc):
    block = block_values.shape[-1]
    scalars, inside = pl.BlockSpec(memory_space=pl.ANY), pl.BlockSpec(memory_space=pltpu.VMEM)
    return pl.pallas_call(
        block_kernel,
        out_shape=(pltpu.VMEM(shared.shape, jnp.float32), pltpu.VMEM(col_acc.shape, jnp.float32)),
        in_specs=[scalars, scalars, inside, inside, pl.BlockSpec(memory_space=pl.ANY), inside, inside],
        out_specs=(inside, inside),
        input_output_aliases={5: 0, 6: 1},
        scratch_shapes=[
            pltpu.VMEM((DEPTH, GROUP, block, block), jnp.int32),
            pltpu.SMEM(coords.shape, jnp.int32),
            pltpu.SMEM(counts.shape, jnp.int32),
            pltpu.SemaphoreType.DMA((DEPTH,)),
            pltpu.SemaphoreType.DMA((2,)),
        ],
        compiler_params=pltpu.CompilerParams(vmem_limit_bytes=12 * 1024 * 1024),
        name="block_terms",
    )(coords, counts, forward, col_all, block_values, shared, col_acc)


REDUCE_SENDS = 60 + 10 + 20
ROW_ORDER = (4, 5, 3, 2, 6, 7, 1)
PASS, SIDE = {1: 0, -1: 1}, {1: 2, -1: 4}


def reduce_kernel(
    shared_ref,
    acc_ref,
    turned_ref,
    cores_ref,
    grad_ref,
    core_total_ref,
    cores,
    low,
    core_terms,
    row_in,
    row_out,
    row_kept,
    col_swap_out,
    col_own,
    col_pair,
    col_in,
    col_out,
    core_out,
    core_in,
    core_y,
    core_z,
    core_all,
    send_sems,
    recv_sems,
    local_sems,
):
    here = Place()
    piece, width = grad_ref.shape
    half_rows, part_rows = piece // 2, piece // 4
    total_rows = turned_ref.shape[1]
    layers, rank, _ = cores_ref.shape
    links = Copies(send_sems, recv_sems, local_sems)
    cores_in = links.local(cores_ref, cores)
    row_count = 2 * RING
    row, col = lax.axis_index("row"), lax.axis_index("col")

    def row_device(d):
        return (lax.rem(row + d, row_count), col)

    partners = [row_device(d) for d in range(1, row_count)]
    partners += [here.device(**{"d" + axis: d}) for axis in "yz" for d in (1, 2, 3)]
    row_part = layers * rank // row_count

    def core_terms_here():
        core_terms[...] = jnp.zeros_like(core_terms)
        step_rows = 8192

        @pl.loop(0, total_rows // step_rows)
        def _(index):
            start = index * step_rows
            own = turned_ref[:, rows(start, step_rows)]
            for layer in range(layers):
                sums = shared_ref[rows(layer * total_rows + start, step_rows)].astype(jnp.bfloat16)
                core_terms[pl.ds(layer * rank, rank)] += dot_nn(own, sums)

        core_out[...] = core_terms[...].astype(jnp.bfloat16)

    greet(partners, core_terms_here)
    halves = (0, 1)
    cores_in.wait()
    for layer in range(layers):
        low[layer] = cores[layer].astype(jnp.bfloat16)

    def term(half, a, b):
        start = here.row_piece(**axes_of(half, a, b)) * piece + half * half_rows
        total = None
        for layer in range(layers):
            sums = shared_ref[rows(layer * total_rows + start, half_rows)].astype(jnp.bfloat16)
            product = dot_nt(sums, low[layer])
            total = product if total is None else total + product
        return total * (1.0 / rank)

    def first(half, sign):
        return here.device(**axes_of(half, sign, 0))

    def second(half, sign):
        return here.device(**axes_of(half, 0, sign))

    def wide(ref):
        return ref[...].astype(jnp.float32)

    def quarter(part):
        return pl.ds(part * part_rows, part_rows)

    def near(sign):
        return 0 if sign == 1 else 1

    sibling = here.device(dcore=1)
    pass_in, side_in, col_swap, stage = {}, {}, {}, {}

    def send_far(a):
        for half in halves:
            both = term(half, a, 2).astype(jnp.bfloat16)
            for sign in (1, -1):
                part = near(sign)
                out = row_out.at[half, a % RING, PASS[sign]]
                out[...] = both[part * part_rows : (part + 1) * part_rows]
                pass_in[half, a, sign] = links.send(
                    out, row_in.at[half, a % RING, PASS[sign]], second(half, sign)
                )

    def send_plain(a):
        for half in halves:
            for sign in (1, -1):
                part = 1 - near(sign)
                both = term(half, a, sign)
                out = row_out.at[half, a % RING, SIDE[sign] + part]
                out[...] = both[part * part_rows : (part + 1) * part_rows].astype(jnp.bfloat16)
                row_kept[half, a % RING, quarter(1 - part)] = both[
                    (1 - part) * part_rows : (2 - part) * part_rows
                ]
                side_in[half, a, sign, part] = links.send(
                    out, row_in.at[half, a % RING, SIDE[sign] + part], second(half, sign)
                )

    def send_sum(a):
        for half in halves:
            for sign in (1, -1):
                part = near(sign)
                mine = row_kept[half, a % RING, quarter(part)]
                pass_in[half, a, sign].wait_recv()
                arrived = wide(row_in.at[half, a % RING, PASS[sign]])
                out = row_out.at[half, a % RING, SIDE[sign] + part]
                out[...] = (mine + arrived).astype(jnp.bfloat16)
                side_in[half, a, sign, part] = links.send(
                    out, row_in.at[half, a % RING, SIDE[sign] + part], second(half, sign)
                )

    def close(a):
        for half in halves:
            mine = term(half, a, 0)
            for part in (0, 1):
                for sign in (1, -1):
                    side_in[half, a, sign, part].wait_recv()
                arrived = wide(row_in.at[half, a % RING, SIDE[1] + part]) + wide(
                    row_in.at[half, a % RING, SIDE[-1] + part]
                )
                row_kept[half, a % RING, pl.ds(part * part_rows, part_rows)] = (
                    mine[part * part_rows : (part + 1) * part_rows] + arrived
                )

    def send_swap(dx):
        slot = dx % RING
        out = col_swap_out.at[slot]
        out[...] = acc_ref[rows(here.col_piece(dx=dx, dcore=1) * piece, piece)].astype(jnp.bfloat16)
        col_swap[dx] = links.send(out, col_pair.at[slot], sibling)

    def core_start():
        for d in ROW_ORDER:
            chunk = lax.rem(row + d, row_count)
            stage["row", d] = links.send(
                core_out.at[rows(chunk * row_part, row_part)], core_in.at[d], row_device(d)
            )

    last_pass, last_in = {}, {}

    def last_out(half, slot, a, part):
        out = row_out.at[half, RING, slot]
        out[...] = row_kept[half, a % RING, pl.ds(part * part_rows, part_rows)].astype(jnp.bfloat16)
        return out

    def last_far():
        for half in halves:
            for sign in (1, -1):
                out = last_out(half, near(sign), 2, near(sign))
                last_pass[half, sign] = links.send(out, row_in.at[half, RING, PASS[sign]], first(half, sign))

    def last_plain(sign):
        for half in halves:
            part = 1 - near(sign)
            out = last_out(half, 2 + part, sign, part)
            last_in[half, sign, part] = links.send(
                out, row_in.at[half, RING, SIDE[sign] + part], first(half, sign)
            )

    def last_sum(sign):
        for half in halves:
            part = near(sign)
            last_pass[half, sign].wait_recv()
            total = row_kept[half, sign % RING, pl.ds(part * part_rows, part_rows)] + wide(
                row_in.at[half, RING, PASS[sign]]
            )
            out = row_out.at[half, RING, 4 + part]
            out[...] = total.astype(jnp.bfloat16)
            last_in[half, sign, part] = links.send(
                out, row_in.at[half, RING, SIDE[sign] + part], first(half, sign)
            )

    col_pass, col_side = {}, {}

    def col_sum(dx):
        mine = acc_ref[rows(here.col_piece(dx=dx) * piece, piece)]
        col_swap[dx].wait_recv()
        return mine + wide(col_pair.at[dx % RING])

    def half_of(part):
        return pl.ds(part * half_rows, half_rows)

    def col_far():
        col_out[0] = col_sum(2).astype(jnp.bfloat16)
        for sign in (1, -1):
            col_pass[sign] = links.send(
                col_out.at[0, half_of(near(sign))], col_in.at[PASS[sign]], here.device(dx=sign)
            )

    def col_plain(sign):
        total = col_sum(sign)
        slot = 1 if sign == 1 else 2
        part = near(sign)
        col_own[slot - 1] = total[part * half_rows : (part + 1) * half_rows]
        part = 1 - near(sign)
        col_out[slot, half_of(part)] = total[part * half_rows : (part + 1) * half_rows].astype(jnp.bfloat16)
        col_side[sign, part] = links.send(
            col_out.at[slot, half_of(part)], col_in.at[SIDE[sign] + part], here.device(dx=sign)
        )

    def col_pass_on(sign):
        slot = 1 if sign == 1 else 2
        part = near(sign)
        col_pass[sign].wait_recv()
        col_out[slot, half_of(part)] = (col_own[slot - 1] + wide(col_in.at[PASS[sign]])).astype(jnp.bfloat16)
        col_side[sign, part] = links.send(
            col_out.at[slot, half_of(part)], col_in.at[SIDE[sign] + part], here.device(dx=sign)
        )

    def col_close():
        total = col_sum(0)
        for part in (0, 1):
            for sign in (1, -1):
                col_side[sign, part].wait_recv()
            grad_ref[half_of(part)] = (
                total[part * half_rows : (part + 1) * half_rows]
                + wide(col_in.at[SIDE[1] + part])
                + wide(col_in.at[SIDE[-1] + part])
            )

    def core_to_y():
        for d in range(1, row_count):
            stage["row", d].wait_recv()
        total = core_terms[rows(row * row_part, row_part)]
        for d in range(1, row_count):
            total += wide(core_in.at[d])
        core_y[here.y] = total.astype(jnp.bfloat16)
        for d in (2, 1, 3):
            stage["y", d] = links.send(core_y.at[here.y], core_y.at[here.y], here.device(dy=d))

    def core_to_z():
        for d in (1, 2, 3):
            stage["y", d].wait_recv()
        total = (wide(core_y.at[0]) + wide(core_y.at[1])) + (wide(core_y.at[2]) + wide(core_y.at[3]))
        core_z[here.z] = total.astype(jnp.bfloat16)
        for d in (2, 1, 3):
            stage["z", d] = links.send(core_z.at[here.z], core_z.at[here.z], here.device(dz=d))

    def core_back_row():
        for d in (1, 2, 3):
            stage["z", d].wait_recv()
        spot = core_all.at[rows(row * row_part, row_part)]
        total = (wide(core_z.at[0]) + wide(core_z.at[1])) + (wide(core_z.at[2]) + wide(core_z.at[3]))
        spot[...] = total.astype(jnp.bfloat16)
        for d in (2, 1, 3):
            stage["bx", d] = links.send(spot, spot, row_device(2 * d))
        stage["chip", 0] = links.send(spot, spot, sibling)

    def core_back_chip():
        for d in (1, 3, 2):
            stage["bx", d].wait_recv()
            from_row = lax.rem(row + 2 * (RING - d), row_count)
            spot = core_all.at[rows(from_row * row_part, row_part)]
            stage["chip", d] = links.send(spot, spot, sibling)

    def core_close():
        for d in range(RING):
            stage["chip", d].wait_recv()
        core_total_ref[...] = wide(core_all)

    core_start()
    send_far(2)
    send_far(1)
    send_far(-1)
    send_far(0)
    send_swap(2)
    send_swap(1)
    send_swap(-1)
    send_swap(0)
    core_to_y()
    send_plain(2)
    send_sum(2)
    send_plain(1)
    core_to_z()
    col_far()
    col_plain(1)
    col_plain(-1)
    send_sum(1)
    send_plain(-1)
    send_plain(0)
    close(2)
    last_far()
    core_back_row()
    send_sum(-1)
    send_sum(0)
    core_back_chip()
    close(1)
    last_plain(1)
    col_pass_on(1)
    col_pass_on(-1)
    links.drain(24)
    close(-1)
    last_plain(-1)
    last_sum(1)
    last_sum(-1)
    col_close()
    core_close()
    close(0)
    links.drain(8)
    for half in halves:
        for part in (0, 1):
            for sign in (1, -1):
                last_in[half, sign, part].wait_recv()
            spot = pl.ds(half * half_rows + part * part_rows, part_rows)
            grad_ref[spot] += (
                row_kept[half, 0, pl.ds(part * part_rows, part_rows)]
                + wide(row_in.at[half, RING, SIDE[1] + part])
                + wide(row_in.at[half, RING, SIDE[-1] + part])
            )
    links.drain()


def reduce(shared, col_acc, turned, cores, piece):
    width = turned.shape[0]
    layers = cores.shape[0]
    half_rows, part_rows = piece // 2, piece // 4
    rank = width
    low, full = jnp.bfloat16, jnp.float32
    anywhere = pl.BlockSpec(memory_space=pl.ANY)
    inside = pl.BlockSpec(memory_space=pltpu.VMEM)
    return pl.pallas_call(
        reduce_kernel,
        out_shape=(
            jax.ShapeDtypeStruct((piece, width), full),
            jax.ShapeDtypeStruct((layers * rank, width), full),
        ),
        in_specs=[inside, inside, inside, anywhere],
        out_specs=(inside, inside),
        scratch_shapes=[
            pltpu.VMEM(cores.shape, full),
            pltpu.VMEM(cores.shape, low),
            pltpu.VMEM((layers * rank, width), full),
            pltpu.VMEM((2, RING + 1, 6, part_rows, width), low),
            pltpu.VMEM((2, RING + 1, 6, part_rows, width), low),
            pltpu.VMEM((2, RING, half_rows, width), full),
            pltpu.VMEM((RING, piece, width), low),
            pltpu.VMEM((2, half_rows, width), full),
            pltpu.VMEM((RING, piece, width), low),
            pltpu.VMEM((6, half_rows, width), low),
            pltpu.VMEM((3, piece, width), low),
            pltpu.VMEM((layers * rank, width), low),
            pltpu.VMEM((2 * RING, layers * rank // (2 * RING), width), low),
            pltpu.VMEM((RING, layers * rank // (2 * RING), width), low),
            pltpu.VMEM((RING, layers * rank // (2 * RING), width), low),
            pltpu.VMEM((layers * rank, width), low),
            pltpu.SemaphoreType.DMA((REDUCE_SENDS,)),
            pltpu.SemaphoreType.DMA((REDUCE_SENDS,)),
            pltpu.SemaphoreType.DMA((1,)),
        ],
        compiler_params=pltpu.CompilerParams(
            collective_id=1, has_side_effects=True, vmem_limit_bytes=18 * 1024 * 1024
        ),
        name="reduce_terms",
    )(shared, col_acc, turned, cores)


def on_device(factor, relation_cores, block_coords, block_values, block_counts):
    slot_count = block_values.shape[3]
    cells = lax.axis_size("row") * lax.axis_size("col")
    layers = relation_cores.shape[0]
    factor_far, cores_far = outside(factor), outside(relation_cores)
    turned, col_all, forward, shared, col_acc = map(pinned, gather(factor_far, cores_far))
    shared, col_acc = map(
        pinned,
        local_terms(
            outside(block_coords.reshape(layers * 2, slot_count)),
            outside(block_counts.reshape(layers)),
            forward,
            col_all,
            block_values,
            shared,
            col_acc,
        ),
    )
    gradient, core_total = reduce(shared, col_acc, turned, cores_far, factor.shape[0])
    factor_next = (factor.astype(jnp.float32) - step_factor * gradient).astype(jnp.bfloat16)
    core_total = core_total.reshape(relation_cores.shape) * (1.0 / factor.shape[1])
    cores_next = relation_cores - step_core / math.sqrt(cells * slot_count) * core_total
    return (factor_next, cores_next)


def solution(mesh):
    placed = (
        P(("row", "col"), None),
        P(),
        P(None, "row", "col", None, None),
        P(None, "row", "col", None, None, None),
        P(None, "row", "col"),
    )
    return jax.shard_map(
        on_device,
        mesh=mesh,
        in_specs=placed,
        out_specs=(P(("row", "col"), None), P()),
        check_vma=False,
    )
```
